128 devices in a mesh: cols: 8 (over z, core), depth: 16 (over x, y).
Axes of the slice: x: 4, y: 4, z: 4, core: 2. Of those that a mesh axis runs over, the one named last changes fastest.
Arguments:
- qtensor: bfloat16 [5, 128, 128, 1024], P(None, 'depth', None, 'cols'), may hold values from -2.5 to 2.5
- labels: int32 [128, 128, 1024], P('depth', None, 'cols'), may hold values from 0 to 3
- tables: float32 [4, 4, 16], replicated, may hold values from 0.2 to 2
Outputs:
- image: float32 [4, 128, 1024], P(None, 'depth', 'cols')
The draws below stay inside these ranges and needn't reach their ends.
All inputs are finite; a program needn't handle non-finite values.
Results may differ from the reference program's by a relative error of at most 0.0003.
Values may be sent and summed in bfloat16 or wider, within the bound.
No kernel may reach another device: no remote copies, remote signals or barrier semaphores. Data moves between devices by JAX's collectives and lax.ppermute only.
A program may use at most 64 MiB of HBM per device.

```python
import math
import jax
import jax.numpy as jnp
from jax import lax

ROWS = 128
LABELS = 4
BINS = 16
NZ = 128
COLS = 1024


def place_ends(values, key, low, largest):
    place = [jax.random.randint(jax.random.fold_in(key, axis), (), 0, length) for axis, length in enumerate(values.shape)]
    widest = values.shape.index(max(values.shape))
    next_to = place[:widest] + [(place[widest] + 1) % values.shape[widest]] + place[widest + 1:]
    return values.at[tuple(place)].set(low).at[tuple(next_to)].set(largest)


def level_of(rng, dims, pieces, smallest, high):
    def one(position, shards_of):
        draws = jax.random.uniform(jax.random.fold_in(jax.random.fold_in(rng, 6), position), (shards_of,), jnp.float32, smallest / len(pieces), high / len(pieces))
        return jnp.repeat(jnp.exp(draws), dims[position] // shards_of).reshape((-1,) + (1,) * (len(dims) - position - 1))

    level = one(*pieces[0])
    for cut in pieces[1:]:
        level = level * one(*cut)
    return level


def noise(own_key, shape, deviation, limit, shards=(), kind=jnp.bfloat16):
    array = deviation * jax.random.normal(own_key, shape, jnp.float32)
    if shards:
        array = array * level_of(own_key, shape, shards, -0.22, 0.18)
    return jnp.clip(array, -limit, limit).astype(kind)


def setup_inputs(seed: int = 0) -> dict:
    streams_of = jax.random.split(jax.random.key(seed), 4)
    qtensor = noise(streams_of[0], (5, NZ, ROWS, COLS), 0.4, 2.5, ((1, 16), (3, 8)))
    labels = place_ends(jax.random.randint(streams_of[1], (NZ, ROWS, COLS), 0, LABELS), jax.random.fold_in(streams_of[1], 1), 0, LABELS - 1).astype(jnp.int32)
    tables = jnp.clip(jnp.exp(jax.random.uniform(streams_of[2], (LABELS, 4, BINS), jnp.float32, math.log(0.2), math.log(2.0))), 0.2, 2.0)
    return {"qtensor": qtensor, "labels": labels, "tables": tables}


def strength_of(q):
    q = q.astype(jnp.float32)
    return 3.0 * (q[0] * q[0] + q[3] * q[3] + q[0] * q[3] + q[1] * q[1] + q[2] * q[2] + q[4] * q[4])


def slope_of(padded):
    dz = (padded[2:, 1:-1, 1:-1] - padded[:-2, 1:-1, 1:-1]) * 0.5
    dy = (padded[1:-1, 2:, 1:-1] - padded[1:-1, :-2, 1:-1]) * 0.5
    dx = (padded[1:-1, 1:-1, 2:] - padded[1:-1, 1:-1, :-2]) * 0.5
    return dz * dz + dy * dy + dx * dx


def shade(strength, slope, labels, tables, step):
    nbins = tables.shape[2]
    nlab = tables.shape[0]
    coord = jnp.clip(2.0 * strength, 0.0, nbins - 1.0)
    masks = [(labels == lab).astype(jnp.float32) for lab in range(nlab)]
    values = [jnp.zeros_like(strength) for chan in range(4)]
    for knot in range(nbins):
        weight = jnp.maximum(0.0, 1.0 - jnp.abs(coord - knot))
        for chan in range(4):
            picked = masks[0] * tables[0, chan, knot]
            for lab in range(1, nlab):
                picked = picked + masks[lab] * tables[lab, chan, knot]
            values[chan] = values[chan] + weight * picked
    extinction = values[3] * (0.25 + slope / (1.0 + slope))
    alpha = 1.0 - jnp.exp(-step * extinction)
    before = jnp.cumsum(extinction, axis=0) - extinction
    transmit = jnp.exp(-step * before)
    weighted = transmit * alpha
    colors = [jnp.sum(weighted * values[chan], axis=0) for chan in range(3)]
    opacity = 1.0 - jnp.exp(-step * jnp.sum(extinction, axis=0))
    return jnp.stack(colors + [opacity], axis=0)


def reference(qtensor, labels, tables):
    depth_all = qtensor.shape[1]
    rows_all = qtensor.shape[2]
    cols_all = qtensor.shape[3]
    step = 2.0 / depth_all
    strength = lax.map(lambda z: strength_of(lax.dynamic_index_in_dim(qtensor, z, 1, keepdims=False)), jnp.arange(depth_all, dtype=jnp.int32))
    padded = jnp.pad(strength, 1)
    width = min(128, cols_all)
    nblocks = cols_all // width

    def one_block(block):
        start = (block * width).astype(jnp.int32)
        sub = lax.dynamic_slice(padded, (jnp.int32(0), jnp.int32(0), start), (depth_all + 2, rows_all + 2, width + 2))
        lab = lax.dynamic_slice(labels, (jnp.int32(0), jnp.int32(0), start), (depth_all, rows_all, width))
        return shade(sub[1:-1, 1:-1, 1:-1], slope_of(sub), lab, tables, step)

    blocks = lax.map(one_block, jnp.arange(nblocks, dtype=jnp.int32))
    return jnp.transpose(blocks, (1, 2, 0, 3)).reshape(4, rows_all, cols_all)
```

```python
import functools
import jax
import jax.numpy as jnp
from jax import lax
from jax.experimental import pallas as pl
from jax.experimental.pallas import tpu as pltpu
from jax.sharding import PartitionSpec as P

LANES = 128
SUB = 8
PAD = 8


def strength_kernel(q_ref, s_ref, first_ref, last_ref, colfirst_ref, collast_ref, edge, edge_t):
    _, nz, rows, lanes = q_ref.shape
    lane = lax.broadcasted_iota(jnp.int32, (16, lanes), 1)
    zeros = jnp.zeros((PAD, lanes), jnp.float32)
    for z in range(nz):
        s_ref[z, 0:PAD, :] = zeros
        s_ref[z, PAD + rows:, :] = zeros

    def block(i, carry):
        r0 = pl.multiple_of(i * 16, 16)
        packed = jnp.zeros((16, lanes), jnp.float32)
        for z in range(nz):
            q = [q_ref[c, z, pl.ds(r0, 16), :].astype(jnp.float32) for c in range(5)]
            s = 3.0 * (q[0] * q[0] + q[3] * q[3] + q[0] * q[3] + q[1] * q[1] + q[2] * q[2] + q[4] * q[4])
            s_ref[z, pl.ds(r0 + PAD, 16), :] = s
            if z == 0:
                first_ref[pl.ds(r0, 16), :] = s
            if z == nz - 1:
                last_ref[pl.ds(r0, 16), :] = s
            turned = pltpu.roll(s, 2 * z + 1, 1)
            packed = jnp.where(lane >> 1 == z, turned, packed)
        edge[pl.ds(r0, 16), :] = packed
        return carry

    lax.fori_loop(0, rows // 16, block, 0)
    edge_t[...] = edge[...].T
    collast_ref[...] = edge_t[pl.ds(0, nz, stride=2), :]
    colfirst_ref[...] = edge_t[pl.ds(1, nz, stride=2), :]


def shade_kernel(step, tab_ref, s_ref, lab_ref, before_ref, after_ref, left_ref, right_ref, out_ref, rows_tab, halo, halo_t):
    nz, rows, lanes = lab_ref.shape
    nlab, nchan, nbins = tab_ref.shape
    d = lax.axis_index("depth")
    c = lax.axis_index("cols")
    has_before = (d > 0).astype(jnp.float32)
    has_after = (d < lax.axis_size("depth") - 1).astype(jnp.float32)
    has_left = (c > 0).astype(jnp.float32)
    has_right = (c < lax.axis_size("cols") - 1).astype(jnp.float32)

    lane = lax.broadcasted_iota(jnp.int32, (SUB, lanes), 1)
    knots = jnp.zeros((SUB, lanes), jnp.float32)
    rows_tab[...] = jnp.zeros_like(rows_tab)
    for lab in range(nlab):
        rows_tab[lab, 0:nchan, 0:nbins] = tab_ref[lab]
    for lab in range(nlab):
        knots = knots + pltpu.roll(rows_tab[lab], lab * nbins, 1)
    delta = pltpu.roll(knots, lanes - 1, 1) - knots
    delta = jnp.where(lane < nlab * nbins, delta, 0.0)
    half = nlab * nbins
    both = knots + pltpu.roll(delta, half, 1)
    table = [jnp.broadcast_to(both[k:k + 1, :], (SUB, lanes)) for k in range(nchan)]

    halo[pl.ds(0, nz, stride=2), :] = left_ref[...] * has_left
    halo[pl.ds(1, nz, stride=2), :] = right_ref[...] * has_right
    halo_t[...] = halo[...].T

    def block(i, carry):
        r0 = pl.multiple_of(i * SUB, SUB)
        at = pl.ds(r0, SUB)
        sides = halo_t[at, :]
        transmit = jnp.ones((SUB, lanes), jnp.float32)
        colors = [jnp.zeros((SUB, lanes), jnp.float32) for _ in range(3)]
        below = before_ref[at, :] * has_before
        here = s_ref[0, pl.ds(r0 + PAD, SUB), :]
        for z in range(nz):
            if z == nz - 1:
                above = after_ref[at, :] * has_after
            else:
                above = s_ref[z + 1, pl.ds(r0 + PAD, SUB), :]
            side = pltpu.roll(sides, lanes - 1 - 2 * z, 1)
            to_left = pltpu.roll(jnp.where(lane == lanes - 1, side, here), 1, 1)
            to_right = pltpu.roll(jnp.where(lane == 0, side, here), lanes - 1, 1)
            dz = above - below
            dx = to_right - to_left
            dy = s_ref[z, pl.ds(r0 + PAD + 1, SUB), :] - s_ref[z, pl.ds(r0 + PAD - 1, SUB), :]
            slope = 0.25 * (dz * dz + dy * dy + dx * dx)
            coord = jnp.clip(2.0 * here, 0.0, nbins - 1.0)
            knot = coord.astype(jnp.int32)
            frac = coord - knot.astype(jnp.float32)
            index = lab_ref[z, at, :] * nbins + knot
            index2 = index + half
            value = []
            for chan in range(nchan):
                base = jnp.take_along_axis(table[chan], index, axis=1, mode="promise_in_bounds")
                diff = jnp.take_along_axis(table[chan], index2, axis=1, mode="promise_in_bounds")
                value.append(base + frac * diff)
            extinction = value[3] * (1.25 - 1.0 / (1.0 + slope))
            passed = transmit * jnp.exp(-step * extinction)
            weight = transmit - passed
            for chan in range(3):
                colors[chan] = colors[chan] + weight * value[chan]
            transmit = passed
            below, here = here, above
        for chan in range(3):
            out_ref[i, chan] = colors[chan]
        out_ref[i, 3] = transmit
        return carry

    lax.fori_loop(0, rows // SUB, block, 0)


def combine_kernel(slab_ref, out_ref):
    count = slab_ref.shape[0]
    transmit = slab_ref[0, 3]
    colors = [slab_ref[0, chan] for chan in range(3)]
    for k in range(1, count):
        for chan in range(3):
            colors[chan] = colors[chan] + transmit * slab_ref[k, chan]
        transmit = transmit * slab_ref[k, 3]
    for chan in range(3):
        out_ref[chan] = colors[chan]
    out_ref[3] = 1.0 - transmit


def on_device(qtensor, labels, tables):
    _, nz, rows, lanes = qtensor.shape
    groups = lax.axis_size("depth")
    across = lax.axis_size("cols")
    step = 2.0 / (nz * groups)
    params = pltpu.CompilerParams(vmem_limit_bytes=32 * 1024 * 1024)
    f32 = lambda *shape: jax.ShapeDtypeStruct(shape, jnp.float32)
    layer = f32(rows, lanes)
    column = f32(nz, rows)
    s, first, last, colfirst, collast = pl.pallas_call(
        strength_kernel,
        out_shape=[f32(nz, rows + 2 * PAD, lanes), layer, layer, column, column],
        scratch_shapes=[pltpu.VMEM((rows, lanes), jnp.float32), pltpu.VMEM((lanes, rows), jnp.float32)],
        compiler_params=params,
        name="strength",
    )(qtensor)

    up = lambda n: [(i, (i + 1) % n) for i in range(n)]
    down = lambda n: [(i, (i - 1) % n) for i in range(n)]
    left = lax.ppermute(collast, "cols", up(across))
    right = lax.ppermute(colfirst, "cols", down(across))
    before = lax.ppermute(last, "depth", up(groups))
    after = lax.ppermute(first, "depth", down(groups))

    slabs = pl.pallas_call(
        functools.partial(shade_kernel, step),
        out_shape=f32(rows // SUB, 4, SUB, lanes),
        scratch_shapes=[
            pltpu.VMEM((tables.shape[0], SUB, lanes), jnp.float32),
            pltpu.VMEM((lanes, rows), jnp.float32),
            pltpu.VMEM((rows, lanes), jnp.float32),
        ],
        compiler_params=params,
        name="shade",
    )(tables, s, labels, before, after, left, right)

    mine = lax.all_to_all(slabs, "depth", 0, 0)
    return pl.pallas_call(
        combine_kernel, out_shape=f32(4, SUB, lanes), compiler_params=params, name="combine"
    )(mine)


def solution(mesh):
    placed = (P(None, "depth", None, "cols"), P("depth", None, "cols"), P())
    return jax.shard_map(
        on_device, mesh=mesh, in_specs=placed, out_specs=P(None, "depth", "cols"), check_vma=False
    )
```

```python
import functools
import jax
import jax.numpy as jnp
from jax import lax
from jax.experimental import pallas as pl
from jax.experimental.pallas import tpu as pltpu
from jax.sharding import PartitionSpec as P

SUB = 8
PAD = 8
CHUNKS = 1
BLOCK = 128


def strength_kernel(q_ref, lab_ref, tab_ref, s_ref, first_ref, last_ref, colfirst_ref, collast_ref, lab_here, knots_ref, q_here, sems, tab_here, rows_tab, edge, edge_t):
    _, nz, rows, lanes = q_here.shape
    part = nz // CHUNKS
    copies = []
    for k in range(CHUNKS):
        at = pl.ds(k * part, part)
        copies.append(pltpu.make_async_copy(q_ref.at[:, at], q_here.at[:, at], sems.at[k]))
        copies[k].start()
    tab_copy = pltpu.make_async_copy(tab_ref, tab_here, sems.at[CHUNKS])
    tab_copy.start()
    lab_copy = pltpu.make_async_copy(lab_ref, lab_here, sems.at[CHUNKS + 1])
    lab_copy.start()
    lane = lax.broadcasted_iota(jnp.int32, (BLOCK, lanes), 1)
    zeros = jnp.zeros((PAD, lanes), jnp.float32)
    for z in range(nz):
        s_ref[z, 0:PAD, :] = zeros
        s_ref[z, PAD + rows:, :] = zeros

    nlab, nchan, nbins = tab_here.shape
    rows_tab[...] = jnp.zeros_like(rows_tab)
    tab_copy.wait()
    for lab in range(nlab):
        rows_tab[lab, 0:nchan, 0:nbins] = tab_here[lab]
    knots = rows_tab[0]
    for lab in range(1, nlab):
        knots = knots + pltpu.roll(rows_tab[lab], lab * nbins, 1)
    knots_ref[0] = knots
    knots_ref[1] = pltpu.roll(knots, lanes - 1, 1) - knots

    for k in range(CHUNKS):
        copies[k].wait()

        def block(i, carry, k=k):
            r0 = pl.multiple_of(i * BLOCK, BLOCK)
            packed = edge[pl.ds(r0, BLOCK), :]
            for z in range(k * part, (k + 1) * part):
                q = [q_here[c, z, pl.ds(r0, BLOCK), :].astype(jnp.float32) for c in range(5)]
                s = 3.0 * (q[0] * q[0] + q[3] * q[3] + q[0] * q[3] + q[1] * q[1] + q[2] * q[2] + q[4] * q[4])
                s_ref[z, pl.ds(r0 + PAD, BLOCK), :] = s
                if z == 0:
                    first_ref[pl.ds(r0, BLOCK), :] = s
                if z == nz - 1:
                    last_ref[pl.ds(r0, BLOCK), :] = s
                turned = pltpu.roll(s, 2 * z + 1, 1)
                packed = jnp.where(lane >> 1 == z, turned, packed)
            edge[pl.ds(r0, BLOCK), :] = packed
            return carry

        lax.fori_loop(0, rows // BLOCK, block, 0)
    edge_t[...] = edge[...].T
    collast_ref[...] = edge_t[pl.ds(0, nz, stride=2), :]
    colfirst_ref[...] = edge_t[pl.ds(1, nz, stride=2), :]
    lab_copy.wait()


def lookup_kernel(nbins, knots_ref, s_ref, lab_ref, value_ref, part_ref, edge_ref):
    nz, rows, lanes = lab_ref.shape
    nchan = value_ref.shape[0]
    lane = lax.broadcasted_iota(jnp.int32, (SUB, lanes), 1)
    inner = (lane > 0) & (lane < lanes - 1)
    base = [jnp.broadcast_to(knots_ref[0, k:k + 1, :], (SUB, lanes)) for k in range(nchan)]
    diff = [jnp.broadcast_to(knots_ref[1, k:k + 1, :], (SUB, lanes)) for k in range(nchan)]

    def block(i, carry):
        r0 = pl.multiple_of(i * SUB, SUB)
        at = pl.ds(r0, SUB)
        packed = jnp.zeros((SUB, lanes), jnp.float32)
        below = None
        here = s_ref[0, pl.ds(r0 + PAD, SUB), :]
        for z in range(nz):
            above = s_ref[z + 1, pl.ds(r0 + PAD, SUB), :] if z < nz - 1 else None
            dx = pltpu.roll(here, lanes - 1, 1) - pltpu.roll(here, 1, 1)
            packed = jnp.where(lane >> 1 == z, pltpu.roll(dx, 2 * z + 1, 1), packed)
            dy = s_ref[z, pl.ds(r0 + PAD + 1, SUB), :] - s_ref[z, pl.ds(r0 + PAD - 1, SUB), :]
            part = dy * dy + jnp.where(inner, dx * dx, 0.0)
            if 0 < z < nz - 1:
                dz = above - below
                part = part + dz * dz
            part_ref[z, at, :] = part
            coord = jnp.clip(2.0 * here, 0.0, nbins - 1.0)
            knot = coord.astype(jnp.int32)
            frac = coord - knot.astype(jnp.float32)
            index = lab_ref[z, at, :] * nbins + knot
            for chan in range(nchan):
                low = jnp.take_along_axis(base[chan], index, axis=1, mode="promise_in_bounds")
                rise = jnp.take_along_axis(diff[chan], index, axis=1, mode="promise_in_bounds")
                value_ref[chan, z, at, :] = low + frac * rise
            below, here = here, above
        edge_ref[at, :] = packed
        return carry

    lax.fori_loop(0, rows // SUB, block, 0)


def finish_kernel(step, value_ref, part_ref, edge_ref, s_ref, colfirst_ref, collast_ref, before_ref, after_ref, left_ref, right_ref,
                  out_ref, halo, halo_t):
    _, nz, rows, lanes = value_ref.shape
    d = lax.axis_index("depth")
    c = lax.axis_index("cols")
    has_before = (d > 0).astype(jnp.float32)
    has_after = (d < lax.axis_size("depth") - 1).astype(jnp.float32)
    has_left = (c > 0).astype(jnp.float32)
    has_right = (c < lax.axis_size("cols") - 1).astype(jnp.float32)
    lane = lax.broadcasted_iota(jnp.int32, (SUB, lanes), 1)
    outer = (lane == 0) | (lane == lanes - 1)

    halo[pl.ds(0, nz, stride=2), :] = right_ref[...] * has_right - colfirst_ref[...]
    halo[pl.ds(1, nz, stride=2), :] = collast_ref[...] - left_ref[...] * has_left
    halo_t[...] = halo[...].T

    def block(i, carry):
        r0 = pl.multiple_of(i * SUB, SUB)
        at = pl.ds(r0, SUB)
        inside = pl.ds(r0 + PAD, SUB)
        sides = halo_t[at, :] + edge_ref[at, :]
        sides = sides * sides
        transmit = jnp.ones((SUB, lanes), jnp.float32)
        colors = [jnp.zeros((SUB, lanes), jnp.float32) for _ in range(3)]
        for z in range(nz):
            slope4 = part_ref[z, at, :] + jnp.where(outer, pltpu.roll(sides, lanes - 1 - 2 * z, 1), 0.0)
            if z == 0:
                dz = s_ref[1, inside, :] - before_ref[at, :] * has_before
                slope4 = slope4 + dz * dz
            if z == nz - 1:
                dz = after_ref[at, :] * has_after - s_ref[nz - 2, inside, :]
                slope4 = slope4 + dz * dz
            extinction = value_ref[3, z, at, :] * (1.25 - 4.0 / (4.0 + slope4))
            passed = transmit * jnp.exp(-step * extinction)
            weight = transmit - passed
            for chan in range(3):
                colors[chan] = colors[chan] + weight * value_ref[chan, z, at, :]
            transmit = passed
        for chan in range(3):
            out_ref[i, chan] = colors[chan]
        out_ref[i, 3] = transmit
        return carry

    lax.fori_loop(0, rows // SUB, block, 0, unroll=2)


def combine_kernel(slab_ref, out_ref):
    count = slab_ref.shape[0]
    transmit = slab_ref[0, 3]
    colors = [slab_ref[0, chan] for chan in range(3)]
    for k in range(1, count):
        for chan in range(3):
            colors[chan] = colors[chan] + transmit * slab_ref[k, chan]
        transmit = transmit * slab_ref[k, 3]
    for chan in range(3):
        out_ref[chan] = colors[chan]
    out_ref[3] = 1.0 - transmit


def on_device(qtensor, labels, tables):
    _, nz, rows, lanes = qtensor.shape
    groups = lax.axis_size("depth")
    across = lax.axis_size("cols")
    step = 2.0 / (nz * groups)
    params = pltpu.CompilerParams(vmem_limit_bytes=32 * 1024 * 1024)
    f32 = lambda *shape: jax.ShapeDtypeStruct(shape, jnp.float32)
    layer = f32(rows, lanes)
    column = f32(nz, rows)
    plane = pltpu.VMEM((rows, lanes), jnp.float32)
    nlab, nchan, nbins = tables.shape
    far = lambda array: pltpu.with_memory_space_constraint(array, pltpu.HBM)
    s, first, last, colfirst, collast, labels, knots = pl.pallas_call(
        strength_kernel,
        in_specs=[pl.BlockSpec(memory_space=pltpu.HBM)] * 3,
        out_shape=[
            f32(nz, rows + 2 * PAD, lanes), layer, layer, column, column,
            jax.ShapeDtypeStruct(labels.shape, labels.dtype), f32(2, SUB, lanes),
        ],
        scratch_shapes=[
            pltpu.VMEM(qtensor.shape, qtensor.dtype),
            pltpu.SemaphoreType.DMA((CHUNKS + 2,)),
            pltpu.VMEM(tables.shape, jnp.float32),
            pltpu.VMEM((nlab, SUB, lanes), jnp.float32),
            plane,
            pltpu.VMEM((lanes, rows), jnp.float32),
        ],
        compiler_params=params,
        name="strength",
    )(far(qtensor), far(labels), far(tables))

    up = lambda n: [(i, (i + 1) % n) for i in range(n)]
    down = lambda n: [(i, (i - 1) % n) for i in range(n)]
    left = lax.ppermute(collast, "cols", up(across))
    right = lax.ppermute(colfirst, "cols", down(across))
    before = lax.ppermute(last, "depth", up(groups))
    after = lax.ppermute(first, "depth", down(groups))

    value, part, edge = pl.pallas_call(
        functools.partial(lookup_kernel, nbins),
        out_shape=[f32(nchan, nz, rows, lanes), f32(nz, rows, lanes), layer],
        compiler_params=params,
        cost_estimate=pl.CostEstimate(flops=60 * nz * rows * lanes, bytes_accessed=28 * nz * rows * lanes, transcendentals=0),
        name="lookup",
    )(knots, s, labels)

    slabs = pl.pallas_call(
        functools.partial(finish_kernel, step),
        out_shape=f32(rows // SUB, 4, SUB, lanes),
        scratch_shapes=[pltpu.VMEM((lanes, rows), jnp.float32), plane],
        compiler_params=params,
        name="finish",
    )(value, part, edge, s, colfirst, collast, before, after, left, right)

    mine = lax.all_to_all(slabs, "depth", 0, 0)
    return pl.pallas_call(
        combine_kernel, out_shape=f32(4, SUB, lanes), compiler_params=params, name="combine"
    )(mine)


def solution(mesh):
    placed = (P(None, "depth", None, "cols"), P("depth", None, "cols"), P())
    return jax.shard_map(
        on_device, mesh=mesh, in_specs=placed, out_specs=P(None, "depth", "cols"), check_vma=False
    )
```

```python
import functools
import jax
import jax.numpy as jnp
from jax import lax
from jax.experimental import pallas as pl
from jax.experimental.pallas import tpu as pltpu
from jax.sharding import PartitionSpec as P

SUB = 8
PAD = 8
CHUNKS = 1
BLOCK = 128


def strength_kernel(q_ref, lab_ref, tab_ref, s_ref, first_ref, last_ref, colfirst_ref, collast_ref, lab_here, knots_ref, q_here, sems, tab_here, rows_tab, edge, edge_t):
    _, nz, rows, lanes = q_here.shape
    part = nz // CHUNKS
    copies = []
    for k in range(CHUNKS):
        at = pl.ds(k * part, part)
        copies.append(pltpu.make_async_copy(q_ref.at[:, at], q_here.at[:, at], sems.at[k]))
        copies[k].start()
    tab_copy = pltpu.make_async_copy(tab_ref, tab_here, sems.at[CHUNKS])
    tab_copy.start()
    lab_copy = pltpu.make_async_copy(lab_ref, lab_here, sems.at[CHUNKS + 1])
    lab_copy.start()
    lane = lax.broadcasted_iota(jnp.int32, (BLOCK, lanes), 1)
    zeros = jnp.zeros((PAD, lanes), jnp.float32)
    for z in range(nz):
        s_ref[z, 0:PAD, :] = zeros
        s_ref[z, PAD + rows:, :] = zeros

    nlab, nchan, nbins = tab_here.shape
    rows_tab[...] = jnp.zeros_like(rows_tab)
    tab_copy.wait()
    for lab in range(nlab):
        rows_tab[lab, 0:nchan, 0:nbins] = tab_here[lab]
    knots = rows_tab[0]
    for lab in range(1, nlab):
        knots = knots + pltpu.roll(rows_tab[lab], lab * nbins, 1)
    knots_ref[0] = knots
    knots_ref[1] = pltpu.roll(knots, lanes - 1, 1) - knots

    for k in range(CHUNKS):
        copies[k].wait()

        def block(i, carry, k=k):
            r0 = pl.multiple_of(i * BLOCK, BLOCK)
            packed = edge[pl.ds(r0, BLOCK), :]
            for z in range(k * part, (k + 1) * part):
                q = [q_here[c, z, pl.ds(r0, BLOCK), :].astype(jnp.float32) for c in range(5)]
                s = 3.0 * (q[0] * q[0] + q[3] * q[3] + q[0] * q[3] + q[1] * q[1] + q[2] * q[2] + q[4] * q[4])
                s_ref[z, pl.ds(r0 + PAD, BLOCK), :] = s
                if z == 0:
                    first_ref[pl.ds(r0, BLOCK), :] = s
                if z == nz - 1:
                    last_ref[pl.ds(r0, BLOCK), :] = s
                turned = pltpu.roll(s, 2 * z + 1, 1)
                packed = jnp.where(lane >> 1 == z, turned, packed)
            edge[pl.ds(r0, BLOCK), :] = packed
            return carry

        lax.fori_loop(0, rows // BLOCK, block, 0)
    edge_t[...] = edge[...].T
    collast_ref[...] = edge_t[pl.ds(0, nz, stride=2), :]
    colfirst_ref[...] = edge_t[pl.ds(1, nz, stride=2), :]
    lab_copy.wait()


def lookup_kernel(nbins, knots_ref, s_ref, lab_ref, value_ref, part_ref, edge_ref):
    nz, rows, lanes = lab_ref.shape
    nchan = value_ref.shape[0]
    lane = lax.broadcasted_iota(jnp.int32, (SUB, lanes), 1)
    inner = (lane > 0) & (lane < lanes - 1)
    base = [jnp.broadcast_to(knots_ref[0, k:k + 1, :], (SUB, lanes)) for k in range(nchan)]
    diff = [jnp.broadcast_to(knots_ref[1, k:k + 1, :], (SUB, lanes)) for k in range(nchan)]

    def block(i, carry):
        r0 = pl.multiple_of(i * SUB, SUB)
        at = pl.ds(r0, SUB)
        packed = jnp.zeros((SUB, lanes), jnp.float32)
        below = None
        here = s_ref[0, pl.ds(r0 + PAD, SUB), :]
        for z in range(nz):
            above = s_ref[z + 1, pl.ds(r0 + PAD, SUB), :] if z < nz - 1 else None
            dx = pltpu.roll(here, lanes - 1, 1) - pltpu.roll(here, 1, 1)
            packed = jnp.where(lane >> 1 == z, pltpu.roll(dx, 2 * z + 1, 1), packed)
            dy = s_ref[z, pl.ds(r0 + PAD + 1, SUB), :] - s_ref[z, pl.ds(r0 + PAD - 1, SUB), :]
            part = dy * dy + jnp.where(inner, dx * dx, 0.0)
            if 0 < z < nz - 1:
                dz = above - below
                part = part + dz * dz
            part_ref[z, at, :] = part
            coord = jnp.clip(2.0 * here, 0.0, nbins - 1.0)
            knot = coord.astype(jnp.int32)
            frac = coord - knot.astype(jnp.float32)
            index = lab_ref[z, at, :] * nbins + knot
            for chan in range(nchan):
                low = jnp.take_along_axis(base[chan], index, axis=1, mode="promise_in_bounds")
                rise = jnp.take_along_axis(diff[chan], index, axis=1, mode="promise_in_bounds")
                value_ref[chan, z, at, :] = low + frac * rise
            below, here = here, above
        edge_ref[at, :] = packed
        return carry

    lax.fori_loop(0, rows // SUB, block, 0)


def finish_kernel(step, value_ref, part_ref, edge_ref, s_ref, colfirst_ref, collast_ref, before_ref, swap1_ref, swap0_ref, after_ref,
                  out_ref, halo, halo_t):
    _, nz, rows, lanes = value_ref.shape
    d = lax.axis_index("depth")
    c = lax.axis_index("cols")
    has_before = (d > 0).astype(jnp.float32)
    has_after = (d < lax.axis_size("depth") - 1).astype(jnp.float32)
    has_left = (c > 0).astype(jnp.float32)
    has_right = (c < lax.axis_size("cols") - 1).astype(jnp.float32)
    lane = lax.broadcasted_iota(jnp.int32, (SUB, lanes), 1)
    outer = (lane == 0) | (lane == lanes - 1)

    odd = c % 2 == 1
    left = jnp.where(odd, swap0_ref[...], swap1_ref[...])
    right = jnp.where(odd, swap1_ref[...], swap0_ref[...])
    halo[pl.ds(0, nz, stride=2), :] = right * has_right - colfirst_ref[...]
    halo[pl.ds(1, nz, stride=2), :] = collast_ref[...] - left * has_left
    halo_t[...] = halo[...].T

    def block(i, carry):
        r0 = pl.multiple_of(i * SUB, SUB)
        at = pl.ds(r0, SUB)
        inside = pl.ds(r0 + PAD, SUB)
        sides = halo_t[at, :] + edge_ref[at, :]
        sides = sides * sides
        transmit = jnp.ones((SUB, lanes), jnp.float32)
        colors = [jnp.zeros((SUB, lanes), jnp.float32) for _ in range(3)]
        for z in range(nz):
            slope4 = part_ref[z, at, :] + jnp.where(outer, pltpu.roll(sides, lanes - 1 - 2 * z, 1), 0.0)
            if z == 0:
                dz = s_ref[1, inside, :] - before_ref[at, :] * has_before
                slope4 = slope4 + dz * dz
            if z == nz - 1:
                dz = after_ref[at, :] * has_after - s_ref[nz - 2, inside, :]
                slope4 = slope4 + dz * dz
            extinction = value_ref[3, z, at, :] * (1.25 - 4.0 / (4.0 + slope4))
            passed = transmit * jnp.exp(-step * extinction)
            weight = transmit - passed
            for chan in range(3):
                colors[chan] = colors[chan] + weight * value_ref[chan, z, at, :]
            transmit = passed
        for chan in range(3):
            out_ref[i, chan] = colors[chan]
        out_ref[i, 3] = transmit
        return carry

    lax.fori_loop(0, rows // SUB, block, 0, unroll=2)


def combine_kernel(slab_ref, out_ref):
    count = slab_ref.shape[0]
    transmit = slab_ref[0, 3]
    colors = [slab_ref[0, chan] for chan in range(3)]
    for k in range(1, count):
        for chan in range(3):
            colors[chan] = colors[chan] + transmit * slab_ref[k, chan]
        transmit = transmit * slab_ref[k, 3]
    for chan in range(3):
        out_ref[chan] = colors[chan]
    out_ref[3] = 1.0 - transmit


def on_device(qtensor, labels, tables):
    _, nz, rows, lanes = qtensor.shape
    groups = lax.axis_size("depth")
    across = lax.axis_size("cols")
    step = 2.0 / (nz * groups)
    params = pltpu.CompilerParams(vmem_limit_bytes=32 * 1024 * 1024)
    f32 = lambda *shape: jax.ShapeDtypeStruct(shape, jnp.float32)
    layer = f32(rows, lanes)
    column = f32(nz, rows)
    plane = pltpu.VMEM((rows, lanes), jnp.float32)
    nlab, nchan, nbins = tables.shape
    far = lambda array: pltpu.with_memory_space_constraint(array, pltpu.HBM)
    s, first, last, colfirst, collast, labels, knots = pl.pallas_call(
        strength_kernel,
        in_specs=[pl.BlockSpec(memory_space=pltpu.HBM)] * 3,
        out_shape=[
            f32(nz, rows + 2 * PAD, lanes), layer, layer, column, column,
            jax.ShapeDtypeStruct(labels.shape, labels.dtype), f32(2, SUB, lanes),
        ],
        scratch_shapes=[
            pltpu.VMEM(qtensor.shape, qtensor.dtype),
            pltpu.SemaphoreType.DMA((CHUNKS + 2,)),
            pltpu.VMEM(tables.shape, jnp.float32),
            pltpu.VMEM((nlab, SUB, lanes), jnp.float32),
            plane,
            pltpu.VMEM((lanes, rows), jnp.float32),
        ],
        compiler_params=params,
        name="strength",
    )(far(qtensor), far(labels), far(tables))

    up = lambda n: [(i, (i + 1) % n) for i in range(n)]
    down = lambda n: [(i, (i - 1) % n) for i in range(n)]
    after = lax.ppermute(first, "depth", down(groups))
    before = lax.ppermute(last, "depth", up(groups))
    c_odd = lax.axis_index("cols") % 2 == 1
    inner = [(i, i ^ 1) for i in range(across)]
    outer = []
    for i in range(across):
        j = ((i + 1) ^ 1) - 1
        for g in range(groups):
            outer.append((i * groups + g, j * groups + g if 0 <= j < across else i * groups + (g ^ 1)))
    swap0 = lax.ppermute(jnp.where(c_odd, colfirst, collast), "cols", inner)
    swap1 = lax.ppermute(jnp.where(c_odd, collast, colfirst), ("cols", "depth"), outer)

    value, part, edge = pl.pallas_call(
        functools.partial(lookup_kernel, nbins),
        out_shape=[f32(nchan, nz, rows, lanes), f32(nz, rows, lanes), layer],
        compiler_params=params,
        cost_estimate=pl.CostEstimate(flops=60 * nz * rows * lanes, bytes_accessed=28 * nz * rows * lanes, transcendentals=0),
        name="lookup",
    )(knots, s, labels)

    slabs = pl.pallas_call(
        functools.partial(finish_kernel, step),
        out_shape=f32(rows // SUB, 4, SUB, lanes),
        scratch_shapes=[pltpu.VMEM((lanes, rows), jnp.float32), plane],
        compiler_params=params,
        name="finish",
    )(value, part, edge, s, colfirst, collast, before, swap1, swap0, after)

    mine = lax.all_to_all(slabs, "depth", 0, 0)
    return pl.pallas_call(
        combine_kernel, out_shape=f32(4, SUB, lanes), compiler_params=params, name="combine"
    )(mine)


def solution(mesh):
    placed = (P(None, "depth", None, "cols"), P("depth", None, "cols"), P())
    return jax.shard_map(
        on_device, mesh=mesh, in_specs=placed, out_specs=P(None, "depth", "cols"), check_vma=False
    )
```

```python
import functools
import jax
import jax.numpy as jnp
from jax import lax
from jax.experimental import pallas as pl
from jax.experimental.pallas import tpu as pltpu
from jax.sharding import PartitionSpec as P

SUB = 8
PAD = 8
CHUNKS = 1
BLOCK = 128
LEVELS = 65535.0
MIDDLE = 32768
MARGIN = 1.0001


def encode(value, scale):
    level = jnp.sqrt(jnp.clip(value / scale, 0.0, 1.0)) * LEVELS + 0.5
    return level.astype(jnp.int32) - MIDDLE


def decode(level, scale):
    root = (level + MIDDLE).astype(jnp.float32) * (1.0 / LEVELS)
    return root * root * scale


def strength_kernel(step, q_ref, lab_ref, tab_ref, s_ref, first_ref, last_ref, colfirst_ref, collast_ref, lab_here, knots_ref, scale_ref, q_here, sems, tab_here, rows_tab, edge, edge_t):
    _, nz, rows, lanes = q_here.shape
    part = nz // CHUNKS
    copies = []
    for k in range(CHUNKS):
        at = pl.ds(k * part, part)
        copies.append(pltpu.make_async_copy(q_ref.at[:, at], q_here.at[:, at], sems.at[k]))
        copies[k].start()
    tab_copy = pltpu.make_async_copy(tab_ref, tab_here, sems.at[CHUNKS])
    tab_copy.start()
    lab_copy = pltpu.make_async_copy(lab_ref, lab_here, sems.at[CHUNKS + 1])
    lab_copy.start()
    lane = lax.broadcasted_iota(jnp.int32, (BLOCK, lanes), 1)
    zeros = jnp.zeros((PAD, lanes), jnp.float32)
    for z in range(nz):
        s_ref[z, 0:PAD, :] = zeros
        s_ref[z, PAD + rows:, :] = zeros

    nlab, nchan, nbins = tab_here.shape
    rows_tab[...] = jnp.zeros_like(rows_tab)
    tab_copy.wait()
    for lab in range(nlab):
        rows_tab[lab, 0:nchan, 0:nbins] = tab_here[lab]
    knots = rows_tab[0]
    for lab in range(1, nlab):
        knots = knots + pltpu.roll(rows_tab[lab], lab * nbins, 1)
    knots_ref[0] = knots
    knots_ref[1] = pltpu.roll(knots, lanes - 1, 1) - knots
    top = jnp.broadcast_to(jnp.max(knots, axis=1, keepdims=True), (SUB, lanes))
    cover = 1.0 - jnp.exp(-1.25 * step * nz * top[nchan - 1:nchan, :])
    row = lax.broadcasted_iota(jnp.int32, (SUB, lanes), 0)
    scale_ref[...] = jnp.where(row < nchan - 1, top, 1.0) * cover * MARGIN

    for k in range(CHUNKS):
        copies[k].wait()

        def block(i, carry, k=k):
            r0 = pl.multiple_of(i * BLOCK, BLOCK)
            packed = edge[pl.ds(r0, BLOCK), :]
            for z in range(k * part, (k + 1) * part):
                q = [q_here[c, z, pl.ds(r0, BLOCK), :].astype(jnp.float32) for c in range(5)]
                s = 3.0 * (q[0] * q[0] + q[3] * q[3] + q[0] * q[3] + q[1] * q[1] + q[2] * q[2] + q[4] * q[4])
                s_ref[z, pl.ds(r0 + PAD, BLOCK), :] = s
                if z == 0:
                    first_ref[pl.ds(r0, BLOCK), :] = s
                if z == nz - 1:
                    last_ref[pl.ds(r0, BLOCK), :] = s
                turned = pltpu.roll(s, 2 * z + 1, 1)
                packed = jnp.where(lane >> 1 == z, turned, packed)
            edge[pl.ds(r0, BLOCK), :] = packed
            return carry

        lax.fori_loop(0, rows // BLOCK, block, 0)
    edge_t[...] = edge[...].T
    collast_ref[...] = edge_t[pl.ds(0, nz, stride=2), :]
    colfirst_ref[...] = edge_t[pl.ds(1, nz, stride=2), :]
    lab_copy.wait()


def lookup_kernel(nbins, knots_ref, s_ref, lab_ref, value_ref, part_ref, edge_ref):
    nz, rows, lanes = lab_ref.shape
    nchan = value_ref.shape[0]
    lane = lax.broadcasted_iota(jnp.int32, (SUB, lanes), 1)
    inner = (lane > 0) & (lane < lanes - 1)
    base = [jnp.broadcast_to(knots_ref[0, k:k + 1, :], (SUB, lanes)) for k in range(nchan)]
    diff = [jnp.broadcast_to(knots_ref[1, k:k + 1, :], (SUB, lanes)) for k in range(nchan)]

    def block(i, carry):
        r0 = pl.multiple_of(i * SUB, SUB)
        at = pl.ds(r0, SUB)
        packed = jnp.zeros((SUB, lanes), jnp.float32)
        below = None
        here = s_ref[0, pl.ds(r0 + PAD, SUB), :]
        for z in range(nz):
            above = s_ref[z + 1, pl.ds(r0 + PAD, SUB), :] if z < nz - 1 else None
            dx = pltpu.roll(here, lanes - 1, 1) - pltpu.roll(here, 1, 1)
            packed = jnp.where(lane >> 1 == z, pltpu.roll(dx, 2 * z + 1, 1), packed)
            dy = s_ref[z, pl.ds(r0 + PAD + 1, SUB), :] - s_ref[z, pl.ds(r0 + PAD - 1, SUB), :]
            part = dy * dy + jnp.where(inner, dx * dx, 0.0)
            if 0 < z < nz - 1:
                dz = above - below
                part = part + dz * dz
            part_ref[z, at, :] = part
            coord = jnp.clip(2.0 * here, 0.0, nbins - 1.0)
            knot = coord.astype(jnp.int32)
            frac = coord - knot.astype(jnp.float32)
            index = lab_ref[z, at, :] * nbins + knot
            for chan in range(nchan):
                low = jnp.take_along_axis(base[chan], index, axis=1, mode="promise_in_bounds")
                rise = jnp.take_along_axis(diff[chan], index, axis=1, mode="promise_in_bounds")
                value_ref[chan, z, at, :] = low + frac * rise
            below, here = here, above
        edge_ref[at, :] = packed
        return carry

    lax.fori_loop(0, rows // SUB, block, 0)


def finish_kernel(step, scale_ref, value_ref, part_ref, edge_ref, s_ref, colfirst_ref, collast_ref, before_ref, swap1_ref, swap0_ref, after_ref,
                  out_ref, halo, halo_t):
    _, nz, rows, lanes = value_ref.shape
    d = lax.axis_index("depth")
    c = lax.axis_index("cols")
    has_before = (d > 0).astype(jnp.float32)
    has_after = (d < lax.axis_size("depth") - 1).astype(jnp.float32)
    has_left = (c > 0).astype(jnp.float32)
    has_right = (c < lax.axis_size("cols") - 1).astype(jnp.float32)
    lane = lax.broadcasted_iota(jnp.int32, (SUB, lanes), 1)
    outer = (lane == 0) | (lane == lanes - 1)

    odd = c % 2 == 1
    left = jnp.where(odd, swap0_ref[...], swap1_ref[...])
    right = jnp.where(odd, swap1_ref[...], swap0_ref[...])
    halo[pl.ds(0, nz, stride=2), :] = right * has_right - colfirst_ref[...]
    halo[pl.ds(1, nz, stride=2), :] = collast_ref[...] - left * has_left
    halo_t[...] = halo[...].T

    scale = [jnp.broadcast_to(scale_ref[k:k + 1, :], (SUB, lanes)) for k in range(4)]

    def block(i, carry):
        r0 = pl.multiple_of(i * SUB, SUB)
        at = pl.ds(r0, SUB)
        inside = pl.ds(r0 + PAD, SUB)
        sides = halo_t[at, :] + edge_ref[at, :]
        sides = sides * sides
        transmit = jnp.ones((SUB, lanes), jnp.float32)
        colors = [jnp.zeros((SUB, lanes), jnp.float32) for _ in range(3)]
        for z in range(nz):
            slope4 = part_ref[z, at, :] + jnp.where(outer, pltpu.roll(sides, lanes - 1 - 2 * z, 1), 0.0)
            if z == 0:
                dz = s_ref[1, inside, :] - before_ref[at, :] * has_before
                slope4 = slope4 + dz * dz
            if z == nz - 1:
                dz = after_ref[at, :] * has_after - s_ref[nz - 2, inside, :]
                slope4 = slope4 + dz * dz
            extinction = value_ref[3, z, at, :] * (1.25 - 4.0 / (4.0 + slope4))
            passed = transmit * jnp.exp(-step * extinction)
            weight = transmit - passed
            for chan in range(3):
                colors[chan] = colors[chan] + weight * value_ref[chan, z, at, :]
            transmit = passed
        sent = [encode(v, scale[k]) for k, v in enumerate(colors + [1.0 - transmit])]
        out_ref[i, 0] = jnp.concatenate(sent[:2], axis=0).astype(jnp.int16)
        out_ref[i, 1] = jnp.concatenate(sent[2:], axis=0).astype(jnp.int16)
        return carry

    lax.fori_loop(0, rows // SUB, block, 0, unroll=8)


def combine_kernel(scale_ref, slab_ref, out_ref):
    count, _, _, lanes = slab_ref.shape
    scale = [jnp.broadcast_to(scale_ref[k:k + 1, :], (SUB, lanes)) for k in range(4)]
    transmit = jnp.ones((SUB, lanes), jnp.float32)
    colors = [jnp.zeros((SUB, lanes), jnp.float32)] * 3
    for k in range(count):
        pairs = [slab_ref[k, j].astype(jnp.int32) for j in range(2)]
        came = [decode(pairs[c // 2][c % 2 * SUB:(c % 2 + 1) * SUB], scale[c]) for c in range(4)]
        for chan in range(3):
            colors[chan] = colors[chan] + transmit * came[chan]
        transmit = transmit * (1.0 - came[3])
    for chan in range(3):
        out_ref[chan] = colors[chan]
    out_ref[3] = 1.0 - transmit


def on_device(qtensor, labels, tables):
    _, nz, rows, lanes = qtensor.shape
    groups = lax.axis_size("depth")
    across = lax.axis_size("cols")
    step = 2.0 / (nz * groups)
    params = pltpu.CompilerParams(vmem_limit_bytes=32 * 1024 * 1024)
    f32 = lambda *shape: jax.ShapeDtypeStruct(shape, jnp.float32)
    layer = f32(rows, lanes)
    column = f32(nz, rows)
    plane = pltpu.VMEM((rows, lanes), jnp.float32)
    nlab, nchan, nbins = tables.shape
    far = lambda array: pltpu.with_memory_space_constraint(array, pltpu.HBM)
    s, first, last, colfirst, collast, labels, knots, scale = pl.pallas_call(
        functools.partial(strength_kernel, step),
        in_specs=[pl.BlockSpec(memory_space=pltpu.HBM)] * 3,
        out_shape=[
            f32(nz, rows + 2 * PAD, lanes), layer, layer, column, column,
            jax.ShapeDtypeStruct(labels.shape, labels.dtype), f32(2, SUB, lanes), f32(SUB, lanes),
        ],
        scratch_shapes=[
            pltpu.VMEM(qtensor.shape, qtensor.dtype),
            pltpu.SemaphoreType.DMA((CHUNKS + 2,)),
            pltpu.VMEM(tables.shape, jnp.float32),
            pltpu.VMEM((nlab, SUB, lanes), jnp.float32),
            plane,
            pltpu.VMEM((lanes, rows), jnp.float32),
        ],
        compiler_params=params,
        name="strength",
    )(far(qtensor), far(labels), far(tables))

    up = lambda n: [(i, (i + 1) % n) for i in range(n)]
    down = lambda n: [(i, (i - 1) % n) for i in range(n)]
    after = lax.ppermute(first, "depth", down(groups))
    before = lax.ppermute(last, "depth", up(groups))
    c_odd = lax.axis_index("cols") % 2 == 1
    inner = [(i, i ^ 1) for i in range(across)]
    outer = []
    for i in range(across):
        j = ((i + 1) ^ 1) - 1
        for g in range(groups):
            outer.append((i * groups + g, j * groups + g if 0 <= j < across else i * groups + (g ^ 1)))
    swap0 = lax.ppermute(jnp.where(c_odd, colfirst, collast), "cols", inner)
    swap1 = lax.ppermute(jnp.where(c_odd, collast, colfirst), ("cols", "depth"), outer)

    value, part, edge = pl.pallas_call(
        functools.partial(lookup_kernel, nbins),
        out_shape=[f32(nchan, nz, rows, lanes), f32(nz, rows, lanes), layer],
        compiler_params=params,
        cost_estimate=pl.CostEstimate(flops=60 * nz * rows * lanes, bytes_accessed=28 * nz * rows * lanes, transcendentals=0),
        name="lookup",
    )(knots, s, labels)

    slabs = pl.pallas_call(
        functools.partial(finish_kernel, step),
        out_shape=jax.ShapeDtypeStruct((rows // SUB, 2, 2 * SUB, lanes), jnp.int16),
        scratch_shapes=[pltpu.VMEM((lanes, rows), jnp.float32), plane],
        compiler_params=params,
        name="finish",
    )(scale, value, part, edge, s, colfirst, collast, before, swap1, swap0, after)

    mine = lax.all_to_all(slabs, "depth", 0, 0)
    return pl.pallas_call(
        combine_kernel, out_shape=f32(4, SUB, lanes), compiler_params=params, name="combine"
    )(scale, mine)


def solution(mesh):
    placed = (P(None, "depth", None, "cols"), P("depth", None, "cols"), P())
    return jax.shard_map(
        on_device, mesh=mesh, in_specs=placed, out_specs=P(None, "depth", "cols"), check_vma=False
    )
```

```python
import functools
import jax
import jax.numpy as jnp
from jax import lax
from jax.experimental import pallas as pl
from jax.experimental.pallas import tpu as pltpu
from jax.sharding import PartitionSpec as P

SUB = 8
PAD = 8
CHUNKS = 1
BLOCK = 128
LEVELS = 65535.0
MIDDLE = 32768
MARGIN = 1.0001


def encode(value, scale):
    level = jnp.sqrt(jnp.clip(value / scale, 0.0, 1.0)) * LEVELS + 0.5
    return level.astype(jnp.int32) - MIDDLE


def decode(level, scale):
    root = (level + MIDDLE).astype(jnp.float32) * (1.0 / LEVELS)
    return root * root * scale


def strength_kernel(step, q_ref, lab_ref, tab_ref, s_ref, first_ref, last_ref, colfirst_ref, collast_ref, lab_here, knots_ref, scale_ref, pick_ref, q_here, sems, tab_here, rows_tab, edge, edge_t):
    _, nz, rows, lanes = q_here.shape
    part = nz // CHUNKS
    copies = []
    for k in range(CHUNKS):
        at = pl.ds(k * part, part)
        copies.append(pltpu.make_async_copy(q_ref.at[:, at], q_here.at[:, at], sems.at[k]))
        copies[k].start()
    tab_copy = pltpu.make_async_copy(tab_ref, tab_here, sems.at[CHUNKS])
    tab_copy.start()
    lab_copy = pltpu.make_async_copy(lab_ref, lab_here, sems.at[CHUNKS + 1])
    lab_copy.start()
    lane = lax.broadcasted_iota(jnp.int32, (BLOCK, lanes), 1)
    zeros = jnp.zeros((PAD, lanes), jnp.float32)
    for z in range(nz):
        s_ref[z, 0:PAD, :] = zeros
        s_ref[z, PAD + rows:, :] = zeros

    nlab, nchan, nbins = tab_here.shape
    rows_tab[...] = jnp.zeros_like(rows_tab)
    tab_copy.wait()
    for lab in range(nlab):
        rows_tab[lab, 0:nchan, 0:nbins] = tab_here[lab]
    knots = rows_tab[0]
    for lab in range(1, nlab):
        knots = knots + pltpu.roll(rows_tab[lab], lab * nbins, 1)
    knots_ref[0] = knots
    knots_ref[1] = pltpu.roll(knots, lanes - 1, 1) - knots
    top = jnp.broadcast_to(jnp.max(knots, axis=1, keepdims=True), (SUB, lanes))
    cover = 1.0 - jnp.exp(-1.25 * step * nz * top[nchan - 1:nchan, :])
    row = lax.broadcasted_iota(jnp.int32, (SUB, lanes), 0)
    scale_ref[...] = jnp.where(row < nchan - 1, top, 1.0) * cover * MARGIN

    src = lax.broadcasted_iota(jnp.int32, (lanes, 2 * lanes), 0)
    dst = lax.broadcasted_iota(jnp.int32, (lanes, 2 * lanes), 1)
    inside = (dst > 0) & (dst < lanes - 1)
    near = jnp.where(inside & (src == dst + 1), 1.0, 0.0) - jnp.where(inside & (src == dst - 1), 1.0, 0.0)
    odd = (dst & 1) == 1
    ends = jnp.where(odd & (src == 1), 1.0, 0.0) - jnp.where(odd, 0.0, jnp.where(src == lanes - 2, 1.0, 0.0))
    pick = jnp.where(dst < lanes, near, ends).astype(jnp.bfloat16)
    pick_ref[0:lanes, :] = pick
    pick_ref[lanes:, :] = pick

    for k in range(CHUNKS):
        copies[k].wait()

        def block(i, carry, k=k):
            r0 = pl.multiple_of(i * BLOCK, BLOCK)
            packed = edge[pl.ds(r0, BLOCK), :]
            for z in range(k * part, (k + 1) * part):
                q = [q_here[c, z, pl.ds(r0, BLOCK), :].astype(jnp.float32) for c in range(5)]
                s = 3.0 * (q[0] * q[0] + q[3] * q[3] + q[0] * q[3] + q[1] * q[1] + q[2] * q[2] + q[4] * q[4])
                s_ref[z, pl.ds(r0 + PAD, BLOCK), :] = s
                if z == 0:
                    first_ref[pl.ds(r0, BLOCK), :] = s
                if z == nz - 1:
                    last_ref[pl.ds(r0, BLOCK), :] = s
                turned = pltpu.roll(s, 2 * z + 1, 1)
                packed = jnp.where(lane >> 1 == z, turned, packed)
            edge[pl.ds(r0, BLOCK), :] = packed
            return carry

        lax.fori_loop(0, rows // BLOCK, block, 0)
    edge_t[...] = edge[...].T
    collast_ref[...] = edge_t[pl.ds(0, nz, stride=2), :]
    colfirst_ref[...] = edge_t[pl.ds(1, nz, stride=2), :]
    lab_copy.wait()


def lookup_kernel(nbins, knots_ref, pick_ref, s_ref, lab_ref, value_ref, part_ref, edge_ref, dx_here):
    nz, rows, lanes = lab_ref.shape
    nchan = value_ref.shape[0]
    lane = lax.broadcasted_iota(jnp.int32, (rows, lanes), 1)
    base = [jnp.broadcast_to(knots_ref[0, k:k + 1, :], (SUB, lanes)) for k in range(nchan)]
    diff = [jnp.broadcast_to(knots_ref[1, k:k + 1, :], (SUB, lanes)) for k in range(nchan)]

    packed = jnp.zeros((rows, lanes), jnp.float32)
    for z in range(nz):
        layer = s_ref[z, PAD:PAD + rows, :]
        high = layer.astype(jnp.bfloat16)
        low = (layer - high.astype(jnp.float32)).astype(jnp.bfloat16)
        both = jnp.dot(jnp.concatenate([high, low], axis=1), pick_ref[...], preferred_element_type=jnp.float32)
        dx_here[z] = both[:, :lanes]
        packed = jnp.where(lane >> 1 == z, both[:, lanes:], packed)
    edge_ref[...] = packed

    def block(i, carry):
        r0 = pl.multiple_of(i * SUB, SUB)
        at = pl.ds(r0, SUB)
        below = None
        here = s_ref[0, pl.ds(r0 + PAD, SUB), :]
        for z in range(nz):
            above = s_ref[z + 1, pl.ds(r0 + PAD, SUB), :] if z < nz - 1 else None
            dx = dx_here[z, at, :]
            dy = s_ref[z, pl.ds(r0 + PAD + 1, SUB), :] - s_ref[z, pl.ds(r0 + PAD - 1, SUB), :]
            part = dy * dy + dx * dx
            if 0 < z < nz - 1:
                dz = above - below
                part = part + dz * dz
            part_ref[z, at, :] = part
            coord = jnp.clip(2.0 * here, 0.0, nbins - 1.0)
            knot = coord.astype(jnp.int32)
            frac = coord - knot.astype(jnp.float32)
            index = lab_ref[z, at, :] * nbins + knot
            for chan in range(nchan):
                low = jnp.take_along_axis(base[chan], index, axis=1, mode="promise_in_bounds")
                rise = jnp.take_along_axis(diff[chan], index, axis=1, mode="promise_in_bounds")
                value_ref[chan, z, at, :] = low + frac * rise
            below, here = here, above
        return carry

    lax.fori_loop(0, rows // SUB, block, 0)


def finish_kernel(step, scale_ref, value_ref, part_ref, edge_ref, s_ref, before_ref, swap1_ref, swap0_ref, after_ref,
                  out_ref, halo, halo_t):
    _, nz, rows, lanes = value_ref.shape
    d = lax.axis_index("depth")
    c = lax.axis_index("cols")
    has_before = (d > 0).astype(jnp.float32)
    has_after = (d < lax.axis_size("depth") - 1).astype(jnp.float32)
    has_left = (c > 0).astype(jnp.float32)
    has_right = (c < lax.axis_size("cols") - 1).astype(jnp.float32)
    lane = lax.broadcasted_iota(jnp.int32, (SUB, lanes), 1)
    outer = (lane == 0) | (lane == lanes - 1)

    odd = c % 2 == 1
    left = jnp.where(odd, swap0_ref[...], swap1_ref[...])
    right = jnp.where(odd, swap1_ref[...], swap0_ref[...])
    halo[pl.ds(0, nz, stride=2), :] = right * has_right
    halo[pl.ds(1, nz, stride=2), :] = -left * has_left
    halo_t[...] = halo[...].T

    scale = [jnp.broadcast_to(scale_ref[k:k + 1, :], (SUB, lanes)) for k in range(4)]

    def block(i, carry):
        r0 = pl.multiple_of(i * SUB, SUB)
        at = pl.ds(r0, SUB)
        inside = pl.ds(r0 + PAD, SUB)
        sides = halo_t[at, :] + edge_ref[at, :]
        sides = sides * sides
        transmit = jnp.ones((SUB, lanes), jnp.float32)
        colors = [jnp.zeros((SUB, lanes), jnp.float32) for _ in range(3)]
        for z in range(nz):
            slope4 = part_ref[z, at, :] + jnp.where(outer, pltpu.roll(sides, lanes - 1 - 2 * z, 1), 0.0)
            if z == 0:
                dz = s_ref[1, inside, :] - before_ref[at, :] * has_before
                slope4 = slope4 + dz * dz
            if z == nz - 1:
                dz = after_ref[at, :] * has_after - s_ref[nz - 2, inside, :]
                slope4 = slope4 + dz * dz
            extinction = value_ref[3, z, at, :] * (1.25 - 4.0 / (4.0 + slope4))
            passed = transmit * jnp.exp(-step * extinction)
            weight = transmit - passed
            for chan in range(3):
                colors[chan] = colors[chan] + weight * value_ref[chan, z, at, :]
            transmit = passed
        sent = [encode(v, scale[k]) for k, v in enumerate(colors + [1.0 - transmit])]
        out_ref[i, 0] = jnp.concatenate(sent[:2], axis=0).astype(jnp.int16)
        out_ref[i, 1] = jnp.concatenate(sent[2:], axis=0).astype(jnp.int16)
        return carry

    lax.fori_loop(0, rows // SUB, block, 0, unroll=8)


def combine_kernel(scale_ref, slab_ref, out_ref):
    count, _, _, lanes = slab_ref.shape
    scale = [jnp.broadcast_to(scale_ref[k:k + 1, :], (SUB, lanes)) for k in range(4)]
    transmit = jnp.ones((SUB, lanes), jnp.float32)
    colors = [jnp.zeros((SUB, lanes), jnp.float32)] * 3
    for k in range(count):
        pairs = [slab_ref[k, j].astype(jnp.int32) for j in range(2)]
        came = [decode(pairs[c // 2][c % 2 * SUB:(c % 2 + 1) * SUB], scale[c]) for c in range(4)]
        for chan in range(3):
            colors[chan] = colors[chan] + transmit * came[chan]
        transmit = transmit * (1.0 - came[3])
    for chan in range(3):
        out_ref[chan] = colors[chan]
    out_ref[3] = 1.0 - transmit


def on_device(qtensor, labels, tables):
    _, nz, rows, lanes = qtensor.shape
    groups = lax.axis_size("depth")
    across = lax.axis_size("cols")
    step = 2.0 / (nz * groups)
    params = pltpu.CompilerParams(vmem_limit_bytes=32 * 1024 * 1024)
    f32 = lambda *shape: jax.ShapeDtypeStruct(shape, jnp.float32)
    layer = f32(rows, lanes)
    column = f32(nz, rows)
    plane = pltpu.VMEM((rows, lanes), jnp.float32)
    nlab, nchan, nbins = tables.shape
    far = lambda array: pltpu.with_memory_space_constraint(array, pltpu.HBM)
    s, first, last, colfirst, collast, labels, knots, scale, pick = pl.pallas_call(
        functools.partial(strength_kernel, step),
        in_specs=[pl.BlockSpec(memory_space=pltpu.HBM)] * 3,
        out_shape=[
            f32(nz, rows + 2 * PAD, lanes), layer, layer, column, column,
            jax.ShapeDtypeStruct(labels.shape, labels.dtype), f32(2, SUB, lanes), f32(SUB, lanes),
            jax.ShapeDtypeStruct((2 * lanes, 2 * lanes), jnp.bfloat16),
        ],
        scratch_shapes=[
            pltpu.VMEM(qtensor.shape, qtensor.dtype),
            pltpu.SemaphoreType.DMA((CHUNKS + 2,)),
            pltpu.VMEM(tables.shape, jnp.float32),
            pltpu.VMEM((nlab, SUB, lanes), jnp.float32),
            plane,
            pltpu.VMEM((lanes, rows), jnp.float32),
        ],
        compiler_params=params,
        name="strength",
    )(far(qtensor), far(labels), far(tables))

    up = lambda n: [(i, (i + 1) % n) for i in range(n)]
    down = lambda n: [(i, (i - 1) % n) for i in range(n)]
    after = lax.ppermute(first, "depth", down(groups))
    before = lax.ppermute(last, "depth", up(groups))
    c_odd = lax.axis_index("cols") % 2 == 1
    inner = [(i, i ^ 1) for i in range(across)]
    outer = []
    for i in range(across):
        j = ((i + 1) ^ 1) - 1
        for g in range(groups):
            outer.append((i * groups + g, j * groups + g if 0 <= j < across else i * groups + (g ^ 1)))
    swap0 = lax.ppermute(jnp.where(c_odd, colfirst, collast), "cols", inner)
    swap1 = lax.ppermute(jnp.where(c_odd, collast, colfirst), ("cols", "depth"), outer)

    value, part, edge = pl.pallas_call(
        functools.partial(lookup_kernel, nbins),
        out_shape=[f32(nchan, nz, rows, lanes), f32(nz, rows, lanes), layer],
        scratch_shapes=[pltpu.VMEM((nz, rows, lanes), jnp.float32)],
        compiler_params=params,
        cost_estimate=pl.CostEstimate(flops=60 * nz * rows * lanes, bytes_accessed=28 * nz * rows * lanes, transcendentals=0),
        name="lookup",
    )(knots, pick, s, labels)

    slabs = pl.pallas_call(
        functools.partial(finish_kernel, step),
        out_shape=jax.ShapeDtypeStruct((rows // SUB, 2, 2 * SUB, lanes), jnp.int16),
        scratch_shapes=[pltpu.VMEM((lanes, rows), jnp.float32), plane],
        compiler_params=params,
        name="finish",
    )(scale, value, part, edge, s, before, swap1, swap0, after)

    mine = lax.all_to_all(slabs, "depth", 0, 0)
    return pl.pallas_call(
        combine_kernel, out_shape=f32(4, SUB, lanes), compiler_params=params, name="combine"
    )(scale, mine)


def solution(mesh):
    placed = (P(None, "depth", None, "cols"), P("depth", None, "cols"), P())
    return jax.shard_map(
        on_device, mesh=mesh, in_specs=placed, out_specs=P(None, "depth", "cols"), check_vma=False
    )
```

```python
import functools
import jax
import jax.numpy as jnp
from jax import lax
from jax.experimental import pallas as pl
from jax.experimental.pallas import tpu as pltpu
from jax.sharding import PartitionSpec as P

SUB = 8
PAD = 8
CHUNKS = 1
BLOCK = 128
LEVELS = 65535.0
MIDDLE = 32768
MARGIN = 1.0001
STRENGTH_MAX = 3.0 * 6.0 * 2.5 * 2.5 * MARGIN


def encode(value, scale):
    level = jnp.sqrt(jnp.clip(value / scale, 0.0, 1.0)) * LEVELS + 0.5
    return level.astype(jnp.int32) - MIDDLE


def decode(level, scale):
    root = (level + MIDDLE).astype(jnp.float32) * (1.0 / LEVELS)
    return root * root * scale


def strength_kernel(step, q_ref, lab_ref, tab_ref, s_ref, first_ref, last_ref, colfirst_ref, collast_ref, lab_here, knots_ref, scale_ref, pick_ref, q_here, sems, tab_here, rows_tab, edge, edge_t):
    _, nz, rows, lanes = q_here.shape
    part = nz // CHUNKS
    copies = []
    for k in range(CHUNKS):
        at = pl.ds(k * part, part)
        copies.append(pltpu.make_async_copy(q_ref.at[:, at], q_here.at[:, at], sems.at[k]))
        copies[k].start()
    tab_copy = pltpu.make_async_copy(tab_ref, tab_here, sems.at[CHUNKS])
    tab_copy.start()
    lab_copy = pltpu.make_async_copy(lab_ref, lab_here, sems.at[CHUNKS + 1])
    lab_copy.start()
    lane = lax.broadcasted_iota(jnp.int32, (BLOCK, lanes), 1)
    zeros = jnp.zeros((PAD, lanes), jnp.float32)
    for z in range(nz):
        s_ref[z, 0:PAD, :] = zeros
        s_ref[z, PAD + rows:, :] = zeros

    nlab, nchan, nbins = tab_here.shape
    rows_tab[...] = jnp.zeros_like(rows_tab)
    tab_copy.wait()
    for lab in range(nlab):
        rows_tab[lab, 0:nchan, 0:nbins] = tab_here[lab]
    knots = rows_tab[0]
    for lab in range(1, nlab):
        knots = knots + pltpu.roll(rows_tab[lab], lab * nbins, 1)
    knots_ref[0] = knots
    knots_ref[1] = pltpu.roll(knots, lanes - 1, 1) - knots
    top = jnp.broadcast_to(jnp.max(knots, axis=1, keepdims=True), (SUB, lanes))
    cover = 1.0 - jnp.exp(-1.25 * step * nz * top[nchan - 1:nchan, :])
    row = lax.broadcasted_iota(jnp.int32, (SUB, lanes), 0)
    scale_ref[...] = jnp.where(row < nchan - 1, top, 1.0) * cover * MARGIN

    src = lax.broadcasted_iota(jnp.int32, (lanes, 2 * lanes), 0)
    dst = lax.broadcasted_iota(jnp.int32, (lanes, 2 * lanes), 1)
    inside = (dst > 0) & (dst < lanes - 1)
    near = jnp.where(inside & (src == dst + 1), 1.0, 0.0) - jnp.where(inside & (src == dst - 1), 1.0, 0.0)
    odd = (dst & 1) == 1
    ends = jnp.where(odd & (src == 1), 1.0, 0.0) - jnp.where(odd, 0.0, jnp.where(src == lanes - 2, 1.0, 0.0))
    pick = jnp.where(dst < lanes, near, ends).astype(jnp.bfloat16)
    pick_ref[0:lanes, :] = pick
    pick_ref[lanes:, :] = pick

    for k in range(CHUNKS):
        copies[k].wait()

        def block(i, carry, k=k):
            r0 = pl.multiple_of(i * BLOCK, BLOCK)
            packed = edge[pl.ds(r0, BLOCK), :]
            for z in range(k * part, (k + 1) * part):
                q = [q_here[c, z, pl.ds(r0, BLOCK), :].astype(jnp.float32) for c in range(5)]
                s = 3.0 * (q[0] * q[0] + q[3] * q[3] + q[0] * q[3] + q[1] * q[1] + q[2] * q[2] + q[4] * q[4])
                s_ref[z, pl.ds(r0 + PAD, BLOCK), :] = s
                if z == 0:
                    first_ref[pl.ds(r0, BLOCK), :] = encode(s, STRENGTH_MAX).astype(jnp.int16)
                if z == nz - 1:
                    last_ref[pl.ds(r0, BLOCK), :] = encode(s, STRENGTH_MAX).astype(jnp.int16)
                turned = pltpu.roll(s, 2 * z + 1, 1)
                packed = jnp.where(lane >> 1 == z, turned, packed)
            edge[pl.ds(r0, BLOCK), :] = packed
            return carry

        lax.fori_loop(0, rows // BLOCK, block, 0)
    edge_t[...] = edge[...].T
    collast_ref[...] = edge_t[pl.ds(0, nz, stride=2), :]
    colfirst_ref[...] = edge_t[pl.ds(1, nz, stride=2), :]
    lab_copy.wait()


def lookup_kernel(nbins, knots_ref, pick_ref, s_ref, lab_ref, value_ref, part_ref, edge_ref, dx_here):
    nz, rows, lanes = lab_ref.shape
    nchan = value_ref.shape[0]
    lane = lax.broadcasted_iota(jnp.int32, (rows, lanes), 1)
    base = [jnp.broadcast_to(knots_ref[0, k:k + 1, :], (SUB, lanes)) for k in range(nchan)]
    diff = [jnp.broadcast_to(knots_ref[1, k:k + 1, :], (SUB, lanes)) for k in range(nchan)]

    packed = jnp.zeros((rows, lanes), jnp.float32)
    for z in range(nz):
        layer = s_ref[z, PAD:PAD + rows, :]
        high = layer.astype(jnp.bfloat16)
        low = (layer - high.astype(jnp.float32)).astype(jnp.bfloat16)
        both = jnp.dot(jnp.concatenate([high, low], axis=1), pick_ref[...], preferred_element_type=jnp.float32)
        dx_here[z] = both[:, :lanes]
        packed = jnp.where(lane >> 1 == z, both[:, lanes:], packed)
    edge_ref[...] = packed

    def block(i, carry):
        r0 = pl.multiple_of(i * SUB, SUB)
        at = pl.ds(r0, SUB)
        below = None
        here = s_ref[0, pl.ds(r0 + PAD, SUB), :]
        for z in range(nz):
            above = s_ref[z + 1, pl.ds(r0 + PAD, SUB), :] if z < nz - 1 else None
            dx = dx_here[z, at, :]
            dy = s_ref[z, pl.ds(r0 + PAD + 1, SUB), :] - s_ref[z, pl.ds(r0 + PAD - 1, SUB), :]
            part = dy * dy + dx * dx
            if 0 < z < nz - 1:
                dz = above - below
                part = part + dz * dz
            part_ref[z, at, :] = part
            coord = jnp.clip(2.0 * here, 0.0, nbins - 1.0)
            knot = coord.astype(jnp.int32)
            frac = coord - knot.astype(jnp.float32)
            index = lab_ref[z, at, :] * nbins + knot
            for chan in range(nchan):
                low = jnp.take_along_axis(base[chan], index, axis=1, mode="promise_in_bounds")
                rise = jnp.take_along_axis(diff[chan], index, axis=1, mode="promise_in_bounds")
                value_ref[chan, z, at, :] = low + frac * rise
            below, here = here, above
        return carry

    lax.fori_loop(0, rows // SUB, block, 0)


def finish_kernel(step, scale_ref, value_ref, part_ref, edge_ref, s_ref, before_ref, swap1_ref, swap0_ref, after_ref,
                  out_ref, halo, halo_t, below_here, above_here):
    _, nz, rows, lanes = value_ref.shape
    d = lax.axis_index("depth")
    c = lax.axis_index("cols")
    has_before = (d > 0).astype(jnp.float32)
    has_after = (d < lax.axis_size("depth") - 1).astype(jnp.float32)
    has_left = (c > 0).astype(jnp.float32)
    has_right = (c < lax.axis_size("cols") - 1).astype(jnp.float32)
    lane = lax.broadcasted_iota(jnp.int32, (SUB, lanes), 1)
    outer = (lane == 0) | (lane == lanes - 1)

    odd = c % 2 == 1
    left = jnp.where(odd, swap0_ref[...], swap1_ref[...])
    right = jnp.where(odd, swap1_ref[...], swap0_ref[...])
    halo[pl.ds(0, nz, stride=2), :] = right * has_right
    halo[pl.ds(1, nz, stride=2), :] = -left * has_left
    halo_t[...] = halo[...].T
    below_here[...] = decode(before_ref[...].astype(jnp.int32), STRENGTH_MAX) * has_before
    above_here[...] = decode(after_ref[...].astype(jnp.int32), STRENGTH_MAX) * has_after

    scale = [jnp.broadcast_to(scale_ref[k:k + 1, :], (SUB, lanes)) for k in range(4)]

    def block(i, carry):
        r0 = pl.multiple_of(i * SUB, SUB)
        at = pl.ds(r0, SUB)
        inside = pl.ds(r0 + PAD, SUB)
        sides = halo_t[at, :] + edge_ref[at, :]
        sides = sides * sides
        transmit = jnp.ones((SUB, lanes), jnp.float32)
        colors = [jnp.zeros((SUB, lanes), jnp.float32) for _ in range(3)]
        for z in range(nz):
            slope4 = part_ref[z, at, :] + jnp.where(outer, pltpu.roll(sides, lanes - 1 - 2 * z, 1), 0.0)
            if z == 0:
                dz = s_ref[1, inside, :] - below_here[at, :]
                slope4 = slope4 + dz * dz
            if z == nz - 1:
                dz = above_here[at, :] - s_ref[nz - 2, inside, :]
                slope4 = slope4 + dz * dz
            extinction = value_ref[3, z, at, :] * (1.25 - 4.0 / (4.0 + slope4))
            passed = transmit * jnp.exp(-step * extinction)
            weight = transmit - passed
            for chan in range(3):
                colors[chan] = colors[chan] + weight * value_ref[chan, z, at, :]
            transmit = passed
        sent = [encode(v, scale[k]) for k, v in enumerate(colors + [1.0 - transmit])]
        out_ref[i, 0] = jnp.concatenate(sent[:2], axis=0).astype(jnp.int16)
        out_ref[i, 1] = jnp.concatenate(sent[2:], axis=0).astype(jnp.int16)
        return carry

    lax.fori_loop(0, rows // SUB, block, 0, unroll=8)


def combine_kernel(scale_ref, slab_ref, out_ref):
    count, _, _, lanes = slab_ref.shape
    scale = [jnp.broadcast_to(scale_ref[k:k + 1, :], (SUB, lanes)) for k in range(4)]
    transmit = jnp.ones((SUB, lanes), jnp.float32)
    colors = [jnp.zeros((SUB, lanes), jnp.float32)] * 3
    for k in range(count):
        pairs = [slab_ref[k, j].astype(jnp.int32) for j in range(2)]
        came = [decode(pairs[c // 2][c % 2 * SUB:(c % 2 + 1) * SUB], scale[c]) for c in range(4)]
        for chan in range(3):
            colors[chan] = colors[chan] + transmit * came[chan]
        transmit = transmit * (1.0 - came[3])
    for chan in range(3):
        out_ref[chan] = colors[chan]
    out_ref[3] = 1.0 - transmit


def on_device(qtensor, labels, tables):
    _, nz, rows, lanes = qtensor.shape
    groups = lax.axis_size("depth")
    across = lax.axis_size("cols")
    step = 2.0 / (nz * groups)
    params = pltpu.CompilerParams(vmem_limit_bytes=32 * 1024 * 1024)
    f32 = lambda *shape: jax.ShapeDtypeStruct(shape, jnp.float32)
    layer = f32(rows, lanes)
    coded = jax.ShapeDtypeStruct((rows, lanes), jnp.int16)
    column = f32(nz, rows)
    plane = pltpu.VMEM((rows, lanes), jnp.float32)
    nlab, nchan, nbins = tables.shape
    far = lambda array: pltpu.with_memory_space_constraint(array, pltpu.HBM)
    s, first, last, colfirst, collast, labels, knots, scale, pick = pl.pallas_call(
        functools.partial(strength_kernel, step),
        in_specs=[pl.BlockSpec(memory_space=pltpu.HBM)] * 3,
        out_shape=[
            f32(nz, rows + 2 * PAD, lanes), coded, coded, column, column,
            jax.ShapeDtypeStruct(labels.shape, labels.dtype), f32(2, SUB, lanes), f32(SUB, lanes),
            jax.ShapeDtypeStruct((2 * lanes, 2 * lanes), jnp.bfloat16),
        ],
        scratch_shapes=[
            pltpu.VMEM(qtensor.shape, qtensor.dtype),
            pltpu.SemaphoreType.DMA((CHUNKS + 2,)),
            pltpu.VMEM(tables.shape, jnp.float32),
            pltpu.VMEM((nlab, SUB, lanes), jnp.float32),
            plane,
            pltpu.VMEM((lanes, rows), jnp.float32),
        ],
        compiler_params=params,
        name="strength",
    )(far(qtensor), far(labels), far(tables))

    up = lambda n: [(i, (i + 1) % n) for i in range(n)]
    down = lambda n: [(i, (i - 1) % n) for i in range(n)]
    after = lax.ppermute(first, "depth", down(groups))
    before = lax.ppermute(last, "depth", up(groups))
    c_odd = lax.axis_index("cols") % 2 == 1
    inner = [(i, i ^ 1) for i in range(across)]
    outer = []
    for i in range(across):
        j = ((i + 1) ^ 1) - 1
        for g in range(groups):
            outer.append((i * groups + g, j * groups + g if 0 <= j < across else i * groups + (g ^ 1)))
    swap0 = lax.ppermute(jnp.where(c_odd, colfirst, collast), "cols", inner)
    swap1 = lax.ppermute(jnp.where(c_odd, collast, colfirst), ("cols", "depth"), outer)

    value, part, edge = pl.pallas_call(
        functools.partial(lookup_kernel, nbins),
        out_shape=[f32(nchan, nz, rows, lanes), f32(nz, rows, lanes), layer],
        scratch_shapes=[pltpu.VMEM((nz, rows, lanes), jnp.float32)],
        compiler_params=params,
        cost_estimate=pl.CostEstimate(flops=60 * nz * rows * lanes, bytes_accessed=28 * nz * rows * lanes, transcendentals=0),
        name="lookup",
    )(knots, pick, s, labels)

    slabs = pl.pallas_call(
        functools.partial(finish_kernel, step),
        out_shape=jax.ShapeDtypeStruct((rows // SUB, 2, 2 * SUB, lanes), jnp.int16),
        scratch_shapes=[pltpu.VMEM((lanes, rows), jnp.float32), plane, plane, plane],
        compiler_params=params,
        name="finish",
    )(scale, value, part, edge, s, before, swap1, swap0, after)

    mine = lax.all_to_all(slabs, "depth", 0, 0)
    return pl.pallas_call(
        combine_kernel, out_shape=f32(4, SUB, lanes), compiler_params=params, name="combine"
    )(scale, mine)


def solution(mesh):
    placed = (P(None, "depth", None, "cols"), P("depth", None, "cols"), P())
    return jax.shard_map(
        on_device, mesh=mesh, in_specs=placed, out_specs=P(None, "depth", "cols"), check_vma=False
    )
```

```python
import functools
import jax
import jax.numpy as jnp
from jax import lax
from jax.experimental import pallas as pl
from jax.experimental.pallas import tpu as pltpu
from jax.sharding import PartitionSpec as P

SUB = 8
PAD = 8
CHUNKS = 2
BLOCK = 128
LEVELS = 65535.0
MIDDLE = 32768
MARGIN = 1.0001
STRENGTH_MAX = 3.0 * 6.0 * 2.5 * 2.5 * MARGIN


def encode(value, scale):
    level = jnp.sqrt(jnp.clip(value / scale, 0.0, 1.0)) * LEVELS + 0.5
    return level.astype(jnp.int32) - MIDDLE


def decode(level, scale):
    root = (level + MIDDLE).astype(jnp.float32) * (1.0 / LEVELS)
    return root * root * scale


def strength_kernel(step, q_ref, lab_ref, tab_ref, s_ref, first_ref, last_ref, colfirst_ref, collast_ref, lab_here, knots_ref, scale_ref, pick_ref, q_here, sems, tab_here, rows_tab, edge, edge_t):
    _, nz, rows, lanes = q_here.shape
    tab_copy = pltpu.make_async_copy(tab_ref, tab_here, sems.at[CHUNKS])
    tab_copy.start()
    part = nz // CHUNKS
    copies = []
    for k in range(CHUNKS):
        at = pl.ds(k * part, part)
        copies.append(pltpu.make_async_copy(q_ref.at[:, at], q_here.at[:, at], sems.at[k]))
        copies[k].start()
    lab_copy = pltpu.make_async_copy(lab_ref, lab_here, sems.at[CHUNKS + 1])
    lab_copy.start()
    lane = lax.broadcasted_iota(jnp.int32, (BLOCK, lanes), 1)
    zeros = jnp.zeros((PAD, lanes), jnp.float32)
    for z in range(nz):
        s_ref[z, 0:PAD, :] = zeros
        s_ref[z, PAD + rows:, :] = zeros

    src = lax.broadcasted_iota(jnp.int32, (lanes, 2 * lanes), 0)
    dst = lax.broadcasted_iota(jnp.int32, (lanes, 2 * lanes), 1)
    inside = (dst > 0) & (dst < lanes - 1)
    near = jnp.where(inside & (src == dst + 1), 1.0, 0.0) - jnp.where(inside & (src == dst - 1), 1.0, 0.0)
    odd = (dst & 1) == 1
    ends = jnp.where(odd & (src == 1), 1.0, 0.0) - jnp.where(odd, 0.0, jnp.where(src == lanes - 2, 1.0, 0.0))
    pick = jnp.where(dst < lanes, near, ends).astype(jnp.bfloat16)
    pick_ref[0:lanes, :] = pick
    pick_ref[lanes:, :] = pick

    nlab, nchan, nbins = tab_here.shape
    rows_tab[...] = jnp.zeros_like(rows_tab)
    tab_copy.wait()
    for lab in range(nlab):
        rows_tab[lab, 0:nchan, 0:nbins] = tab_here[lab]
    knots = rows_tab[0]
    for lab in range(1, nlab):
        knots = knots + pltpu.roll(rows_tab[lab], lab * nbins, 1)
    knots_ref[0] = knots
    knots_ref[1] = pltpu.roll(knots, lanes - 1, 1) - knots
    top = jnp.broadcast_to(jnp.max(knots, axis=1, keepdims=True), (SUB, lanes))
    cover = 1.0 - jnp.exp(-1.25 * step * nz * top[nchan - 1:nchan, :])
    row = lax.broadcasted_iota(jnp.int32, (SUB, lanes), 0)
    scale_ref[...] = jnp.where(row < nchan - 1, top, 1.0) * cover * MARGIN

    for k in range(CHUNKS):
        copies[k].wait()

        def block(i, carry, k=k):
            r0 = pl.multiple_of(i * BLOCK, BLOCK)
            packed = edge[pl.ds(r0, BLOCK), :]
            for z in range(k * part, (k + 1) * part):
                q = [q_here[c, z, pl.ds(r0, BLOCK), :].astype(jnp.float32) for c in range(5)]
                s = 3.0 * (q[0] * q[0] + q[3] * q[3] + q[0] * q[3] + q[1] * q[1] + q[2] * q[2] + q[4] * q[4])
                s_ref[z, pl.ds(r0 + PAD, BLOCK), :] = s
                if z == 0:
                    first_ref[pl.ds(r0, BLOCK), :] = encode(s, STRENGTH_MAX).astype(jnp.int16)
                if z == nz - 1:
                    last_ref[pl.ds(r0, BLOCK), :] = encode(s, STRENGTH_MAX).astype(jnp.int16)
                turned = pltpu.roll(s, 2 * z + 1, 1)
                packed = jnp.where(lane >> 1 == z, turned, packed)
            edge[pl.ds(r0, BLOCK), :] = packed
            return carry

        lax.fori_loop(0, rows // BLOCK, block, 0)
    edge_t[...] = edge[...].T
    collast_ref[...] = edge_t[pl.ds(0, nz, stride=2), :]
    colfirst_ref[...] = edge_t[pl.ds(1, nz, stride=2), :]
    lab_copy.wait()


def lookup_kernel(nbins, knots_ref, pick_ref, s_ref, lab_ref, value_ref, part_ref, edge_ref, dx_here):
    nz, rows, lanes = lab_ref.shape
    nchan = value_ref.shape[0]
    lane = lax.broadcasted_iota(jnp.int32, (rows, lanes), 1)
    base = [jnp.broadcast_to(knots_ref[0, k:k + 1, :], (SUB, lanes)) for k in range(nchan)]
    diff = [jnp.broadcast_to(knots_ref[1, k:k + 1, :], (SUB, lanes)) for k in range(nchan)]

    packed = jnp.zeros((rows, lanes), jnp.float32)
    for z in range(nz):
        layer = s_ref[z, PAD:PAD + rows, :]
        high = layer.astype(jnp.bfloat16)
        low = (layer - high.astype(jnp.float32)).astype(jnp.bfloat16)
        both = jnp.dot(jnp.concatenate([high, low], axis=1), pick_ref[...], preferred_element_type=jnp.float32)
        dx_here[z] = both[:, :lanes]
        packed = jnp.where(lane >> 1 == z, both[:, lanes:], packed)
    edge_ref[...] = packed

    def block(i, carry):
        r0 = pl.multiple_of(i * SUB, SUB)
        at = pl.ds(r0, SUB)
        below = None
        here = s_ref[0, pl.ds(r0 + PAD, SUB), :]
        for z in range(nz):
            above = s_ref[z + 1, pl.ds(r0 + PAD, SUB), :] if z < nz - 1 else None
            dx = dx_here[z, at, :]
            dy = s_ref[z, pl.ds(r0 + PAD + 1, SUB), :] - s_ref[z, pl.ds(r0 + PAD - 1, SUB), :]
            part = dy * dy + dx * dx
            if 0 < z < nz - 1:
                dz = above - below
                part = part + dz * dz
            part_ref[z, at, :] = part
            coord = jnp.clip(2.0 * here, 0.0, nbins - 1.0)
            knot = coord.astype(jnp.int32)
            frac = coord - knot.astype(jnp.float32)
            index = lab_ref[z, at, :] * nbins + knot
            for chan in range(nchan):
                low = jnp.take_along_axis(base[chan], index, axis=1, mode="promise_in_bounds")
                rise = jnp.take_along_axis(diff[chan], index, axis=1, mode="promise_in_bounds")
                value_ref[chan, z, at, :] = low + frac * rise
            below, here = here, above
        return carry

    lax.fori_loop(0, rows // SUB, block, 0)


def finish_kernel(step, scale_ref, value_ref, part_ref, edge_ref, s_ref, before_ref, swap1_ref, swap0_ref, after_ref,
                  out_ref, halo, halo_t, below_here, above_here):
    _, nz, rows, lanes = value_ref.shape
    d = lax.axis_index("depth")
    c = lax.axis_index("cols")
    has_before = (d > 0).astype(jnp.float32)
    has_after = (d < lax.axis_size("depth") - 1).astype(jnp.float32)
    has_left = (c > 0).astype(jnp.float32)
    has_right = (c < lax.axis_size("cols") - 1).astype(jnp.float32)
    lane = lax.broadcasted_iota(jnp.int32, (SUB, lanes), 1)
    outer = (lane == 0) | (lane == lanes - 1)

    odd = c % 2 == 1
    left = jnp.where(odd, swap0_ref[...], swap1_ref[...])
    right = jnp.where(odd, swap1_ref[...], swap0_ref[...])
    halo[pl.ds(0, nz, stride=2), :] = right * has_right
    halo[pl.ds(1, nz, stride=2), :] = -left * has_left
    halo_t[...] = halo[...].T
    below_here[...] = decode(before_ref[...].astype(jnp.int32), STRENGTH_MAX) * has_before
    above_here[...] = decode(after_ref[...].astype(jnp.int32), STRENGTH_MAX) * has_after

    scale = [jnp.broadcast_to(scale_ref[k:k + 1, :], (SUB, lanes)) for k in range(4)]

    def block(i, carry):
        r0 = pl.multiple_of(i * SUB, SUB)
        at = pl.ds(r0, SUB)
        inside = pl.ds(r0 + PAD, SUB)
        sides = halo_t[at, :] + edge_ref[at, :]
        sides = sides * sides
        transmit = jnp.ones((SUB, lanes), jnp.float32)
        colors = [jnp.zeros((SUB, lanes), jnp.float32) for _ in range(3)]
        for z in range(nz):
            slope4 = part_ref[z, at, :] + jnp.where(outer, pltpu.roll(sides, lanes - 1 - 2 * z, 1), 0.0)
            if z == 0:
                dz = s_ref[1, inside, :] - below_here[at, :]
                slope4 = slope4 + dz * dz
            if z == nz - 1:
                dz = above_here[at, :] - s_ref[nz - 2, inside, :]
                slope4 = slope4 + dz * dz
            extinction = value_ref[3, z, at, :] * (1.25 - 4.0 / (4.0 + slope4))
            passed = transmit * jnp.exp(-step * extinction)
            weight = transmit - passed
            for chan in range(3):
                colors[chan] = colors[chan] + weight * value_ref[chan, z, at, :]
            transmit = passed
        sent = [encode(v, scale[k]) for k, v in enumerate(colors + [1.0 - transmit])]
        out_ref[i, 0] = jnp.concatenate(sent[:2], axis=0).astype(jnp.int16)
        out_ref[i, 1] = jnp.concatenate(sent[2:], axis=0).astype(jnp.int16)
        return carry

    lax.fori_loop(0, rows // SUB, block, 0, unroll=8)


def combine_kernel(scale_ref, slab_ref, out_ref):
    count, _, _, lanes = slab_ref.shape
    scale = [jnp.broadcast_to(scale_ref[k:k + 1, :], (SUB, lanes)) for k in range(4)]
    transmit = jnp.ones((SUB, lanes), jnp.float32)
    colors = [jnp.zeros((SUB, lanes), jnp.float32)] * 3
    for k in range(count):
        pairs = [slab_ref[k, j].astype(jnp.int32) for j in range(2)]
        came = [decode(pairs[c // 2][c % 2 * SUB:(c % 2 + 1) * SUB], scale[c]) for c in range(4)]
        for chan in range(3):
            colors[chan] = colors[chan] + transmit * came[chan]
        transmit = transmit * (1.0 - came[3])
    for chan in range(3):
        out_ref[chan] = colors[chan]
    out_ref[3] = 1.0 - transmit


def on_device(qtensor, labels, tables):
    _, nz, rows, lanes = qtensor.shape
    groups = lax.axis_size("depth")
    across = lax.axis_size("cols")
    step = 2.0 / (nz * groups)
    params = pltpu.CompilerParams(vmem_limit_bytes=32 * 1024 * 1024)
    f32 = lambda *shape: jax.ShapeDtypeStruct(shape, jnp.float32)
    layer = f32(rows, lanes)
    coded = jax.ShapeDtypeStruct((rows, lanes), jnp.int16)
    column = f32(nz, rows)
    plane = pltpu.VMEM((rows, lanes), jnp.float32)
    nlab, nchan, nbins = tables.shape
    far = lambda array: pltpu.with_memory_space_constraint(array, pltpu.HBM)
    s, first, last, colfirst, collast, labels, knots, scale, pick = pl.pallas_call(
        functools.partial(strength_kernel, step),
        in_specs=[pl.BlockSpec(memory_space=pltpu.HBM)] * 3,
        out_shape=[
            f32(nz, rows + 2 * PAD, lanes), coded, coded, column, column,
            jax.ShapeDtypeStruct(labels.shape, labels.dtype), f32(2, SUB, lanes), f32(SUB, lanes),
            jax.ShapeDtypeStruct((2 * lanes, 2 * lanes), jnp.bfloat16),
        ],
        scratch_shapes=[
            pltpu.VMEM(qtensor.shape, qtensor.dtype),
            pltpu.SemaphoreType.DMA((CHUNKS + 2,)),
            pltpu.VMEM(tables.shape, jnp.float32),
            pltpu.VMEM((nlab, SUB, lanes), jnp.float32),
            plane,
            pltpu.VMEM((lanes, rows), jnp.float32),
        ],
        compiler_params=params,
        name="strength",
    )(far(qtensor), far(labels), far(tables))

    up = lambda n: [(i, (i + 1) % n) for i in range(n)]
    down = lambda n: [(i, (i - 1) % n) for i in range(n)]
    after = lax.ppermute(first, "depth", down(groups))
    before = lax.ppermute(last, "depth", up(groups))
    c_odd = lax.axis_index("cols") % 2 == 1
    inner = [(i, i ^ 1) for i in range(across)]
    outer = []
    for i in range(across):
        j = ((i + 1) ^ 1) - 1
        for g in range(groups):
            outer.append((i * groups + g, j * groups + g if 0 <= j < across else i * groups + (g ^ 1)))
    swap0 = lax.ppermute(jnp.where(c_odd, colfirst, collast), "cols", inner)
    swap1 = lax.ppermute(jnp.where(c_odd, collast, colfirst), ("cols", "depth"), outer)

    value, part, edge = pl.pallas_call(
        functools.partial(lookup_kernel, nbins),
        out_shape=[f32(nchan, nz, rows, lanes), f32(nz, rows, lanes), layer],
        scratch_shapes=[pltpu.VMEM((nz, rows, lanes), jnp.float32)],
        compiler_params=params,
        cost_estimate=pl.CostEstimate(flops=60 * nz * rows * lanes, bytes_accessed=28 * nz * rows * lanes, transcendentals=0),
        name="lookup",
    )(knots, pick, s, labels)

    slabs = pl.pallas_call(
        functools.partial(finish_kernel, step),
        out_shape=jax.ShapeDtypeStruct((rows // SUB, 2, 2 * SUB, lanes), jnp.int16),
        scratch_shapes=[pltpu.VMEM((lanes, rows), jnp.float32), plane, plane, plane],
        compiler_params=params,
        name="finish",
    )(scale, value, part, edge, s, before, swap1, swap0, after)

    mine = lax.all_to_all(slabs, "depth", 0, 0)
    return pl.pallas_call(
        combine_kernel, out_shape=f32(4, SUB, lanes), compiler_params=params, name="combine"
    )(scale, mine)


def solution(mesh):
    placed = (P(None, "depth", None, "cols"), P("depth", None, "cols"), P())
    return jax.shard_map(
        on_device, mesh=mesh, in_specs=placed, out_specs=P(None, "depth", "cols"), check_vma=False
    )
```

```python
import functools
import jax
import jax.numpy as jnp
from jax import lax
from jax.experimental import pallas as pl
from jax.experimental.pallas import tpu as pltpu
from jax.sharding import PartitionSpec as P

SUB = 8
PAD = 8
CHUNKS = 2
BLOCK = 128
LEVELS = 65535.0
MIDDLE = 32768
MARGIN = 1.0001
STRENGTH_MAX = 3.0 * 6.0 * 2.5 * 2.5 * MARGIN


def encode(value, scale):
    level = jnp.sqrt(jnp.clip(value / scale, 0.0, 1.0)) * LEVELS + 0.5
    return level.astype(jnp.int32) - MIDDLE


def decode(level, scale):
    root = (level + MIDDLE).astype(jnp.float32) * (1.0 / LEVELS)
    return root * root * scale


def strength_kernel(step, q_ref, lab_ref, tab_ref, s_ref, first_ref, last_ref, colfirst_ref, collast_ref, lab_here, knots_ref, scale_ref, pick_ref, q_here, sems, tab_here, rows_tab, edge, edge_t):
    _, nz, rows, lanes = q_here.shape
    tab_copy = pltpu.make_async_copy(tab_ref, tab_here, sems.at[CHUNKS])
    tab_copy.start()
    part = nz // CHUNKS
    copies = []
    for k in range(CHUNKS):
        at = pl.ds(k * part, part)
        copies.append(pltpu.make_async_copy(q_ref.at[:, at], q_here.at[:, at], sems.at[k]))
        copies[k].start()
    lab_copy = pltpu.make_async_copy(lab_ref, lab_here, sems.at[CHUNKS + 1])
    lab_copy.start()
    lane = lax.broadcasted_iota(jnp.int32, (BLOCK, lanes), 1)
    zeros = jnp.zeros((PAD, lanes), jnp.float32)
    for z in range(nz):
        s_ref[z, 0:PAD, :] = zeros
        s_ref[z, PAD + rows:, :] = zeros

    src = lax.broadcasted_iota(jnp.int32, (lanes, 2 * lanes), 0)
    dst = lax.broadcasted_iota(jnp.int32, (lanes, 2 * lanes), 1)
    inside = (dst > 0) & (dst < lanes - 1)
    near = jnp.where(inside & (src == dst + 1), 1.0, 0.0) - jnp.where(inside & (src == dst - 1), 1.0, 0.0)
    odd = (dst & 1) == 1
    ends = jnp.where(odd & (src == 1), 1.0, 0.0) - jnp.where(odd, 0.0, jnp.where(src == lanes - 2, 1.0, 0.0))
    pick = jnp.where(dst < lanes, near, ends).astype(jnp.bfloat16)
    pick_ref[0:lanes, :] = pick
    pick_ref[lanes:, :] = pick

    nlab, nchan, nbins = tab_here.shape
    rows_tab[...] = jnp.zeros_like(rows_tab)
    tab_copy.wait()
    for lab in range(nlab):
        rows_tab[lab, 0:nchan, 0:nbins] = tab_here[lab]
    knots = rows_tab[0]
    for lab in range(1, nlab):
        knots = knots + pltpu.roll(rows_tab[lab], lab * nbins, 1)
    knots_ref[0] = knots
    knots_ref[1] = pltpu.roll(knots, lanes - 1, 1) - knots
    top = jnp.broadcast_to(jnp.max(knots, axis=1, keepdims=True), (SUB, lanes))
    cover = 1.0 - jnp.exp(-1.25 * step * nz * top[nchan - 1:nchan, :])
    row = lax.broadcasted_iota(jnp.int32, (SUB, lanes), 0)
    scale_ref[...] = jnp.where(row < nchan - 1, top, 1.0) * cover * MARGIN

    for k in range(CHUNKS):
        copies[k].wait()

        def block(i, carry, k=k):
            r0 = pl.multiple_of(i * BLOCK, BLOCK)
            packed = edge[pl.ds(r0, BLOCK), :]
            for z in range(k * part, (k + 1) * part):
                q = [q_here[c, z, pl.ds(r0, BLOCK), :].astype(jnp.float32) for c in range(5)]
                s = 3.0 * (q[0] * q[0] + q[3] * q[3] + q[0] * q[3] + q[1] * q[1] + q[2] * q[2] + q[4] * q[4])
                s_ref[z, pl.ds(r0 + PAD, BLOCK), :] = s
                if z == 0:
                    first_ref[pl.ds(r0, BLOCK), :] = encode(s, STRENGTH_MAX).astype(jnp.int16)
                if z == nz - 1:
                    last_ref[pl.ds(r0, BLOCK), :] = encode(s, STRENGTH_MAX).astype(jnp.int16)
                turned = pltpu.roll(s, 2 * z + 1, 1)
                packed = jnp.where(lane >> 1 == z, turned, packed)
            edge[pl.ds(r0, BLOCK), :] = packed
            return carry

        lax.fori_loop(0, rows // BLOCK, block, 0)
    edge_t[...] = edge[...].T
    collast_ref[...] = edge_t[pl.ds(0, nz, stride=2), :]
    colfirst_ref[...] = edge_t[pl.ds(1, nz, stride=2), :]
    lab_copy.wait()


def lookup_kernel(nbins, knots_ref, pick_ref, s_ref, lab_ref, value_ref, part_ref, edge_ref, dx_here):
    nz, rows, lanes = lab_ref.shape
    nchan = value_ref.shape[0]
    lane = lax.broadcasted_iota(jnp.int32, (rows, lanes), 1)
    base = [jnp.broadcast_to(knots_ref[0, k:k + 1, :], (SUB, lanes)) for k in range(nchan)]
    diff = [jnp.broadcast_to(knots_ref[1, k:k + 1, :], (SUB, lanes)) for k in range(nchan)]

    packed = jnp.zeros((rows, lanes), jnp.float32)
    for z in range(nz):
        layer = s_ref[z, PAD:PAD + rows, :]
        high = layer.astype(jnp.bfloat16)
        low = (layer - high.astype(jnp.float32)).astype(jnp.bfloat16)
        both = jnp.dot(jnp.concatenate([high, low], axis=1), pick_ref[...], preferred_element_type=jnp.float32)
        dx_here[z] = both[:, :lanes]
        packed = jnp.where(lane >> 1 == z, both[:, lanes:], packed)
    edge_ref[...] = packed

    def block(i, carry):
        r0 = pl.multiple_of(i * SUB, SUB)
        at = pl.ds(r0, SUB)
        below = None
        here = s_ref[0, pl.ds(r0 + PAD, SUB), :]
        for z in range(nz):
            above = s_ref[z + 1, pl.ds(r0 + PAD, SUB), :] if z < nz - 1 else None
            dx = dx_here[z, at, :]
            dy = s_ref[z, pl.ds(r0 + PAD + 1, SUB), :] - s_ref[z, pl.ds(r0 + PAD - 1, SUB), :]
            part = dy * dy + dx * dx
            if 0 < z < nz - 1:
                dz = above - below
                part = part + dz * dz
            part_ref[z, at, :] = part
            coord = jnp.clip(2.0 * here, 0.0, nbins - 1.0)
            knot = coord.astype(jnp.int32)
            frac = coord - knot.astype(jnp.float32)
            index = lab_ref[z, at, :] * nbins + knot
            for chan in range(nchan):
                low = jnp.take_along_axis(base[chan], index, axis=1, mode="promise_in_bounds")
                rise = jnp.take_along_axis(diff[chan], index, axis=1, mode="promise_in_bounds")
                value_ref[chan, z, at, :] = low + frac * rise
            below, here = here, above
        return carry

    lax.fori_loop(0, rows // SUB, block, 0, unroll=4)


def finish_kernel(step, scale_ref, value_ref, part_ref, edge_ref, s_ref, before_ref, swap1_ref, swap0_ref, after_ref,
                  out_ref, halo, halo_t, below_here, above_here):
    _, nz, rows, lanes = value_ref.shape
    d = lax.axis_index("depth")
    c = lax.axis_index("cols")
    has_before = (d > 0).astype(jnp.float32)
    has_after = (d < lax.axis_size("depth") - 1).astype(jnp.float32)
    has_left = (c > 0).astype(jnp.float32)
    has_right = (c < lax.axis_size("cols") - 1).astype(jnp.float32)
    lane = lax.broadcasted_iota(jnp.int32, (SUB, lanes), 1)
    outer = (lane == 0) | (lane == lanes - 1)

    odd = c % 2 == 1
    left = jnp.where(odd, swap0_ref[...], swap1_ref[...])
    right = jnp.where(odd, swap1_ref[...], swap0_ref[...])
    halo[pl.ds(0, nz, stride=2), :] = right * has_right
    halo[pl.ds(1, nz, stride=2), :] = -left * has_left
    halo_t[...] = halo[...].T
    below_here[...] = decode(before_ref[...].astype(jnp.int32), STRENGTH_MAX) * has_before
    above_here[...] = decode(after_ref[...].astype(jnp.int32), STRENGTH_MAX) * has_after

    scale = [jnp.broadcast_to(scale_ref[k:k + 1, :], (SUB, lanes)) for k in range(4)]

    def block(i, carry):
        r0 = pl.multiple_of(i * SUB, SUB)
        at = pl.ds(r0, SUB)
        inside = pl.ds(r0 + PAD, SUB)
        sides = halo_t[at, :] + edge_ref[at, :]
        sides = sides * sides
        transmit = jnp.ones((SUB, lanes), jnp.float32)
        colors = [jnp.zeros((SUB, lanes), jnp.float32) for _ in range(3)]
        for z in range(nz):
            slope4 = part_ref[z, at, :] + jnp.where(outer, pltpu.roll(sides, lanes - 1 - 2 * z, 1), 0.0)
            if z == 0:
                dz = s_ref[1, inside, :] - below_here[at, :]
                slope4 = slope4 + dz * dz
            if z == nz - 1:
                dz = above_here[at, :] - s_ref[nz - 2, inside, :]
                slope4 = slope4 + dz * dz
            extinction = value_ref[3, z, at, :] * (1.25 - 4.0 / (4.0 + slope4))
            passed = transmit * jnp.exp(-step * extinction)
            weight = transmit - passed
            for chan in range(3):
                colors[chan] = colors[chan] + weight * value_ref[chan, z, at, :]
            transmit = passed
        sent = [encode(v, scale[k]) for k, v in enumerate(colors + [1.0 - transmit])]
        out_ref[i, 0] = jnp.concatenate(sent[:2], axis=0).astype(jnp.int16)
        out_ref[i, 1] = jnp.concatenate(sent[2:], axis=0).astype(jnp.int16)
        return carry

    lax.fori_loop(0, rows // SUB, block, 0, unroll=16)


def combine_kernel(scale_ref, slab_ref, out_ref):
    count, _, _, lanes = slab_ref.shape
    scale = [jnp.broadcast_to(scale_ref[k:k + 1, :], (SUB, lanes)) for k in range(4)]
    transmit = jnp.ones((SUB, lanes), jnp.float32)
    colors = [jnp.zeros((SUB, lanes), jnp.float32)] * 3
    for k in range(count):
        pairs = [slab_ref[k, j].astype(jnp.int32) for j in range(2)]
        came = [decode(pairs[c // 2][c % 2 * SUB:(c % 2 + 1) * SUB], scale[c]) for c in range(4)]
        for chan in range(3):
            colors[chan] = colors[chan] + transmit * came[chan]
        transmit = transmit * (1.0 - came[3])
    for chan in range(3):
        out_ref[chan] = colors[chan]
    out_ref[3] = 1.0 - transmit


def on_device(qtensor, labels, tables):
    _, nz, rows, lanes = qtensor.shape
    groups = lax.axis_size("depth")
    across = lax.axis_size("cols")
    step = 2.0 / (nz * groups)
    params = pltpu.CompilerParams(vmem_limit_bytes=32 * 1024 * 1024)
    f32 = lambda *shape: jax.ShapeDtypeStruct(shape, jnp.float32)
    layer = f32(rows, lanes)
    coded = jax.ShapeDtypeStruct((rows, lanes), jnp.int16)
    column = f32(nz, rows)
    plane = pltpu.VMEM((rows, lanes), jnp.float32)
    nlab, nchan, nbins = tables.shape
    far = lambda array: pltpu.with_memory_space_constraint(array, pltpu.HBM)
    s, first, last, colfirst, collast, labels, knots, scale, pick = pl.pallas_call(
        functools.partial(strength_kernel, step),
        in_specs=[pl.BlockSpec(memory_space=pltpu.HBM)] * 3,
        out_shape=[
            f32(nz, rows + 2 * PAD, lanes), coded, coded, column, column,
            jax.ShapeDtypeStruct(labels.shape, labels.dtype), f32(2, SUB, lanes), f32(SUB, lanes),
            jax.ShapeDtypeStruct((2 * lanes, 2 * lanes), jnp.bfloat16),
        ],
        scratch_shapes=[
            pltpu.VMEM(qtensor.shape, qtensor.dtype),
            pltpu.SemaphoreType.DMA((CHUNKS + 2,)),
            pltpu.VMEM(tables.shape, jnp.float32),
            pltpu.VMEM((nlab, SUB, lanes), jnp.float32),
            plane,
            pltpu.VMEM((lanes, rows), jnp.float32),
        ],
        compiler_params=params,
        name="strength",
    )(far(qtensor), far(labels), far(tables))

    up = lambda n: [(i, (i + 1) % n) for i in range(n)]
    down = lambda n: [(i, (i - 1) % n) for i in range(n)]
    after = lax.ppermute(first, "depth", down(groups))
    before = lax.ppermute(last, "depth", up(groups))
    c_odd = lax.axis_index("cols") % 2 == 1
    inner = [(i, i ^ 1) for i in range(across)]
    outer = []
    for i in range(across):
        j = ((i + 1) ^ 1) - 1
        for g in range(groups):
            outer.append((i * groups + g, j * groups + g if 0 <= j < across else i * groups + (g ^ groups // 4)))
    swap0 = lax.ppermute(jnp.where(c_odd, colfirst, collast), "cols", inner)
    swap1 = lax.ppermute(jnp.where(c_odd, collast, colfirst), ("cols", "depth"), outer)

    value, part, edge = pl.pallas_call(
        functools.partial(lookup_kernel, nbins),
        out_shape=[f32(nchan, nz, rows, lanes), f32(nz, rows, lanes), layer],
        scratch_shapes=[pltpu.VMEM((nz, rows, lanes), jnp.float32)],
        compiler_params=params,
        cost_estimate=pl.CostEstimate(flops=60 * nz * rows * lanes, bytes_accessed=28 * nz * rows * lanes, transcendentals=0),
        name="lookup",
    )(knots, pick, s, labels)

    slabs = pl.pallas_call(
        functools.partial(finish_kernel, step),
        out_shape=jax.ShapeDtypeStruct((rows // SUB, 2, 2 * SUB, lanes), jnp.int16),
        scratch_shapes=[pltpu.VMEM((lanes, rows), jnp.float32), plane, plane, plane],
        compiler_params=params,
        name="finish",
    )(scale, value, part, edge, s, before, swap1, swap0, after)

    mine = lax.all_to_all(slabs, "depth", 0, 0)
    return pl.pallas_call(
        combine_kernel, out_shape=f32(4, SUB, lanes), compiler_params=params, name="combine"
    )(scale, mine)


def solution(mesh):
    placed = (P(None, "depth", None, "cols"), P("depth", None, "cols"), P())
    return jax.shard_map(
        on_device, mesh=mesh, in_specs=placed, out_specs=P(None, "depth", "cols"), check_vma=False
    )
```

```python
import functools
import jax
import jax.numpy as jnp
from jax import lax
from jax.experimental import pallas as pl
from jax.experimental.pallas import tpu as pltpu
from jax.sharding import PartitionSpec as P

SUB = 8
PAD = 8
CHUNKS = 2
BLOCK = 128
LEVELS = 65535.0
MIDDLE = 32768
MARGIN = 1.0001
STRENGTH_MAX = 3.0 * 6.0 * 2.5 * 2.5 * MARGIN


def encode(value, scale):
    level = jnp.sqrt(jnp.clip(value / scale, 0.0, 1.0)) * LEVELS + 0.5
    return level.astype(jnp.int32) - MIDDLE


def decode(level, scale):
    root = (level + MIDDLE).astype(jnp.float32) * (1.0 / LEVELS)
    return root * root * scale


def strength_kernel(step, q_ref, lab_ref, tab_ref, s_ref, first_ref, last_ref, colfirst_ref, collast_ref, lab_here, knots_ref, scale_ref, pick_ref, q_here, sems, tab_here, rows_tab, edge, edge_t):
    _, nz, rows, lanes = q_here.shape
    tab_copy = pltpu.make_async_copy(tab_ref, tab_here, sems.at[CHUNKS])
    tab_copy.start()
    part = nz // CHUNKS
    copies = []
    for k in range(CHUNKS):
        at = pl.ds(k * part, part)
        copies.append(pltpu.make_async_copy(q_ref.at[:, at], q_here.at[:, at], sems.at[k]))
        copies[k].start()
    lab_copy = pltpu.make_async_copy(lab_ref, lab_here, sems.at[CHUNKS + 1])
    lab_copy.start()
    lane = lax.broadcasted_iota(jnp.int32, (BLOCK, lanes), 1)
    zeros = jnp.zeros((PAD, lanes), jnp.float32)
    for z in range(nz):
        s_ref[z, 0:PAD, :] = zeros
        s_ref[z, PAD + rows:, :] = zeros

    src = lax.broadcasted_iota(jnp.int32, (lanes, 2 * lanes), 0)
    dst = lax.broadcasted_iota(jnp.int32, (lanes, 2 * lanes), 1)
    inside = (dst > 0) & (dst < lanes - 1)
    near = jnp.where(inside & (src == dst + 1), 1.0, 0.0) - jnp.where(inside & (src == dst - 1), 1.0, 0.0)
    odd = (dst & 1) == 1
    ends = jnp.where(odd & (src == 1), 1.0, 0.0) - jnp.where(odd, 0.0, jnp.where(src == lanes - 2, 1.0, 0.0))
    pick = jnp.where(dst < lanes, near, ends).astype(jnp.bfloat16)
    pick_ref[0:lanes, :] = pick
    pick_ref[lanes:, :] = pick

    nlab, nchan, nbins = tab_here.shape
    rows_tab[...] = jnp.zeros_like(rows_tab)
    tab_copy.wait()
    for lab in range(nlab):
        rows_tab[lab, 0:nchan, 0:nbins] = tab_here[lab]
    knots = rows_tab[0]
    for lab in range(1, nlab):
        knots = knots + pltpu.roll(rows_tab[lab], lab * nbins, 1)
    knots_ref[0] = knots
    knots_ref[1] = pltpu.roll(knots, lanes - 1, 1) - knots
    top = jnp.broadcast_to(jnp.max(knots, axis=1, keepdims=True), (SUB, lanes))
    cover = 1.0 - jnp.exp(-1.25 * step * nz * top[nchan - 1:nchan, :])
    row = lax.broadcasted_iota(jnp.int32, (SUB, lanes), 0)
    scale_ref[...] = jnp.where(row < nchan - 1, top, 1.0) * cover * MARGIN

    for k in range(CHUNKS):
        copies[k].wait()

        def block(i, carry, k=k):
            r0 = pl.multiple_of(i * BLOCK, BLOCK)
            packed = edge[pl.ds(r0, BLOCK), :]
            for z in range(k * part, (k + 1) * part):
                q = [q_here[c, z, pl.ds(r0, BLOCK), :].astype(jnp.float32) for c in range(5)]
                s = 3.0 * (q[0] * q[0] + q[3] * q[3] + q[0] * q[3] + q[1] * q[1] + q[2] * q[2] + q[4] * q[4])
                s_ref[z, pl.ds(r0 + PAD, BLOCK), :] = s
                if z == 0:
                    first_ref[pl.ds(r0, BLOCK), :] = encode(s, STRENGTH_MAX).astype(jnp.int16)
                if z == nz - 1:
                    last_ref[pl.ds(r0, BLOCK), :] = encode(s, STRENGTH_MAX).astype(jnp.int16)
                turned = pltpu.roll(s, 2 * z + 1, 1)
                packed = jnp.where(lane >> 1 == z, turned, packed)
            edge[pl.ds(r0, BLOCK), :] = packed
            return carry

        lax.fori_loop(0, rows // BLOCK, block, 0)
    edge_t[...] = edge[...].T
    collast_ref[...] = edge_t[pl.ds(0, nz, stride=2), :]
    colfirst_ref[...] = edge_t[pl.ds(1, nz, stride=2), :]
    lab_copy.wait()


def lookup_kernel(nbins, knots_ref, pick_ref, s_ref, lab_ref, value_ref, part_ref, edge_ref, dx_here):
    nz, rows, lanes = lab_ref.shape
    nchan = value_ref.shape[0]
    lane = lax.broadcasted_iota(jnp.int32, (rows, lanes), 1)
    base = [jnp.broadcast_to(knots_ref[0, k:k + 1, :], (SUB, lanes)) for k in range(nchan)]
    diff = [jnp.broadcast_to(knots_ref[1, k:k + 1, :], (SUB, lanes)) for k in range(nchan)]

    packed = jnp.zeros((rows, lanes), jnp.float32)
    for z in range(nz):
        layer = s_ref[z, PAD:PAD + rows, :]
        high = layer.astype(jnp.bfloat16)
        low = (layer - high.astype(jnp.float32)).astype(jnp.bfloat16)
        both = jnp.dot(jnp.concatenate([high, low], axis=1), pick_ref[...], preferred_element_type=jnp.float32)
        dx_here[z] = both[:, :lanes]
        packed = jnp.where(lane >> 1 == z, both[:, lanes:], packed)
    edge_ref[...] = packed

    def block(i, carry):
        r0 = pl.multiple_of(i * SUB, SUB)
        at = pl.ds(r0, SUB)
        below = None
        here = s_ref[0, pl.ds(r0 + PAD, SUB), :]
        for z in range(nz):
            above = s_ref[z + 1, pl.ds(r0 + PAD, SUB), :] if z < nz - 1 else None
            dx = dx_here[z, at, :]
            dy = s_ref[z, pl.ds(r0 + PAD + 1, SUB), :] - s_ref[z, pl.ds(r0 + PAD - 1, SUB), :]
            part = dy * dy + dx * dx
            if 0 < z < nz - 1:
                dz = above - below
                part = part + dz * dz
            part_ref[z, at, :] = part
            coord = jnp.clip(2.0 * here, 0.0, nbins - 1.0)
            knot = coord.astype(jnp.int32)
            frac = coord - knot.astype(jnp.float32)
            index = lab_ref[z, at, :] * nbins + knot
            for chan in range(nchan):
                low = jnp.take_along_axis(base[chan], index, axis=1, mode="promise_in_bounds")
                rise = jnp.take_along_axis(diff[chan], index, axis=1, mode="promise_in_bounds")
                value_ref[chan, z, at, :] = low + frac * rise
            below, here = here, above
        return carry

    lax.fori_loop(0, rows // SUB, block, 0, unroll=4)


def most_kernel(step, value_ref, part_ref, edge_ref, s_ref, before_ref, swap1_ref, swap0_ref,
                state_ref, slope_ref, halo, halo_t, below_here):
    _, nz, rows, lanes = value_ref.shape
    d = lax.axis_index("depth")
    c = lax.axis_index("cols")
    has_before = (d > 0).astype(jnp.float32)
    has_left = (c > 0).astype(jnp.float32)
    has_right = (c < lax.axis_size("cols") - 1).astype(jnp.float32)
    lane = lax.broadcasted_iota(jnp.int32, (SUB, lanes), 1)
    outer = (lane == 0) | (lane == lanes - 1)

    odd = c % 2 == 1
    left = jnp.where(odd, swap0_ref[...], swap1_ref[...])
    right = jnp.where(odd, swap1_ref[...], swap0_ref[...])
    halo[pl.ds(0, nz, stride=2), :] = right * has_right
    halo[pl.ds(1, nz, stride=2), :] = -left * has_left
    halo_t[...] = halo[...].T
    below_here[...] = decode(before_ref[...].astype(jnp.int32), STRENGTH_MAX) * has_before


    def block(i, carry):
        r0 = pl.multiple_of(i * SUB, SUB)
        at = pl.ds(r0, SUB)
        inside = pl.ds(r0 + PAD, SUB)
        sides = halo_t[at, :] + edge_ref[at, :]
        sides = sides * sides
        transmit = jnp.ones((SUB, lanes), jnp.float32)
        colors = [jnp.zeros((SUB, lanes), jnp.float32) for _ in range(3)]
        for z in range(nz):
            slope4 = part_ref[z, at, :] + jnp.where(outer, pltpu.roll(sides, lanes - 1 - 2 * z, 1), 0.0)
            if z == 0:
                dz = s_ref[1, inside, :] - below_here[at, :]
                slope4 = slope4 + dz * dz
            if z == nz - 1:
                slope_ref[at, :] = slope4
                break
            extinction = value_ref[3, z, at, :] * (1.25 - 4.0 / (4.0 + slope4))
            passed = transmit * jnp.exp(-step * extinction)
            weight = transmit - passed
            for chan in range(3):
                colors[chan] = colors[chan] + weight * value_ref[chan, z, at, :]
            transmit = passed
        for k, v in enumerate(colors + [transmit]):
            state_ref[i, k] = v
        return carry

    lax.fori_loop(0, rows // SUB, block, 0, unroll=16)


def last_kernel(step, scale_ref, state_ref, slope_ref, value_ref, s_ref, after_ref, out_ref, above_here):
    _, nz, rows, lanes = value_ref.shape
    has_after = (lax.axis_index("depth") < lax.axis_size("depth") - 1).astype(jnp.float32)
    above_here[...] = decode(after_ref[...].astype(jnp.int32), STRENGTH_MAX) * has_after
    scale = [jnp.broadcast_to(scale_ref[k:k + 1, :], (SUB, lanes)) for k in range(4)]

    def block(i, carry):
        r0 = pl.multiple_of(i * SUB, SUB)
        at = pl.ds(r0, SUB)
        dz = above_here[at, :] - s_ref[nz - 2, pl.ds(r0 + PAD, SUB), :]
        slope4 = slope_ref[at, :] + dz * dz
        extinction = value_ref[3, nz - 1, at, :] * (1.25 - 4.0 / (4.0 + slope4))
        transmit = state_ref[i, 3]
        passed = transmit * jnp.exp(-step * extinction)
        weight = transmit - passed
        colors = [state_ref[i, chan] + weight * value_ref[chan, nz - 1, at, :] for chan in range(3)]
        sent = [encode(v, scale[k]) for k, v in enumerate(colors + [1.0 - passed])]
        out_ref[i, 0] = jnp.concatenate(sent[:2], axis=0).astype(jnp.int16)
        out_ref[i, 1] = jnp.concatenate(sent[2:], axis=0).astype(jnp.int16)
        return carry

    lax.fori_loop(0, rows // SUB, block, 0, unroll=16)


def combine_kernel(scale_ref, slab_ref, out_ref):
    count, _, _, lanes = slab_ref.shape
    scale = [jnp.broadcast_to(scale_ref[k:k + 1, :], (SUB, lanes)) for k in range(4)]
    transmit = jnp.ones((SUB, lanes), jnp.float32)
    colors = [jnp.zeros((SUB, lanes), jnp.float32)] * 3
    for k in range(count):
        pairs = [slab_ref[k, j].astype(jnp.int32) for j in range(2)]
        came = [decode(pairs[c // 2][c % 2 * SUB:(c % 2 + 1) * SUB], scale[c]) for c in range(4)]
        for chan in range(3):
            colors[chan] = colors[chan] + transmit * came[chan]
        transmit = transmit * (1.0 - came[3])
    for chan in range(3):
        out_ref[chan] = colors[chan]
    out_ref[3] = 1.0 - transmit


def on_device(qtensor, labels, tables):
    _, nz, rows, lanes = qtensor.shape
    groups = lax.axis_size("depth")
    across = lax.axis_size("cols")
    step = 2.0 / (nz * groups)
    params = pltpu.CompilerParams(vmem_limit_bytes=32 * 1024 * 1024)
    f32 = lambda *shape: jax.ShapeDtypeStruct(shape, jnp.float32)
    layer = f32(rows, lanes)
    coded = jax.ShapeDtypeStruct((rows, lanes), jnp.int16)
    column = f32(nz, rows)
    plane = pltpu.VMEM((rows, lanes), jnp.float32)
    nlab, nchan, nbins = tables.shape
    far = lambda array: pltpu.with_memory_space_constraint(array, pltpu.HBM)
    s, first, last, colfirst, collast, labels, knots, scale, pick = pl.pallas_call(
        functools.partial(strength_kernel, step),
        in_specs=[pl.BlockSpec(memory_space=pltpu.HBM)] * 3,
        out_shape=[
            f32(nz, rows + 2 * PAD, lanes), coded, coded, column, column,
            jax.ShapeDtypeStruct(labels.shape, labels.dtype), f32(2, SUB, lanes), f32(SUB, lanes),
            jax.ShapeDtypeStruct((2 * lanes, 2 * lanes), jnp.bfloat16),
        ],
        scratch_shapes=[
            pltpu.VMEM(qtensor.shape, qtensor.dtype),
            pltpu.SemaphoreType.DMA((CHUNKS + 2,)),
            pltpu.VMEM(tables.shape, jnp.float32),
            pltpu.VMEM((nlab, SUB, lanes), jnp.float32),
            plane,
            pltpu.VMEM((lanes, rows), jnp.float32),
        ],
        compiler_params=params,
        name="strength",
    )(far(qtensor), far(labels), far(tables))

    up = lambda n: [(i, (i + 1) % n) for i in range(n)]
    down = lambda n: [(i, (i - 1) % n) for i in range(n)]
    after = lax.ppermute(first, "depth", down(groups))
    before = lax.ppermute(last, "depth", up(groups))
    c_odd = lax.axis_index("cols") % 2 == 1
    inner = [(i, i ^ 1) for i in range(across)]
    outer = []
    for i in range(across):
        j = ((i + 1) ^ 1) - 1
        for g in range(groups):
            outer.append((i * groups + g, j * groups + g if 0 <= j < across else i * groups + (g ^ groups // 4)))
    swap0 = lax.ppermute(jnp.where(c_odd, colfirst, collast), "cols", inner)
    swap1 = lax.ppermute(jnp.where(c_odd, collast, colfirst), ("cols", "depth"), outer)

    value, part, edge = pl.pallas_call(
        functools.partial(lookup_kernel, nbins),
        out_shape=[f32(nchan, nz, rows, lanes), f32(nz, rows, lanes), layer],
        scratch_shapes=[pltpu.VMEM((nz, rows, lanes), jnp.float32)],
        compiler_params=params,
        cost_estimate=pl.CostEstimate(flops=60 * nz * rows * lanes, bytes_accessed=28 * nz * rows * lanes, transcendentals=0),
        name="lookup",
    )(knots, pick, s, labels)

    state, slope = pl.pallas_call(
        functools.partial(most_kernel, step),
        out_shape=[f32(rows // SUB, 4, SUB, lanes), layer],
        scratch_shapes=[pltpu.VMEM((lanes, rows), jnp.float32), plane, plane],
        compiler_params=params,
        name="most",
    )(value, part, edge, s, before, swap1, swap0)
    slabs = pl.pallas_call(
        functools.partial(last_kernel, step),
        out_shape=jax.ShapeDtypeStruct((rows // SUB, 2, 2 * SUB, lanes), jnp.int16),
        scratch_shapes=[plane],
        compiler_params=params,
        name="last",
    )(scale, state, slope, value, s, after)

    mine = lax.all_to_all(slabs, "depth", 0, 0)
    return pl.pallas_call(
        combine_kernel, out_shape=f32(4, SUB, lanes), compiler_params=params, name="combine"
    )(scale, mine)


def solution(mesh):
    placed = (P(None, "depth", None, "cols"), P("depth", None, "cols"), P())
    return jax.shard_map(
        on_device, mesh=mesh, in_specs=placed, out_specs=P(None, "depth", "cols"), check_vma=False
    )
```

```python
import functools
import jax
import jax.numpy as jnp
from jax import lax
from jax.experimental import pallas as pl
from jax.experimental.pallas import tpu as pltpu
from jax.sharding import PartitionSpec as P

SUB = 8
PAD = 8
CHUNKS = 2
BLOCK = 128
LEVELS = 65535.0
MIDDLE = 32768
MARGIN = 1.0001
STRENGTH_MAX = 3.0 * 6.0 * 2.5 * 2.5 * MARGIN


def encode(value, scale):
    level = jnp.sqrt(jnp.clip(value / scale, 0.0, 1.0)) * LEVELS + 0.5
    return level.astype(jnp.int32) - MIDDLE


def decode(level, scale):
    root = (level + MIDDLE).astype(jnp.float32) * (1.0 / LEVELS)
    return root * root * scale


def strength_kernel(step, q_ref, lab_ref, tab_ref, s_ref, first_ref, last_ref, inner_ref, outer_ref, lab_here, knots_ref, scale_ref, pick_ref, q_here, sems, tab_here, rows_tab, edge, edge_t):
    _, nz, rows, lanes = q_here.shape
    tab_copy = pltpu.make_async_copy(tab_ref, tab_here, sems.at[CHUNKS])
    tab_copy.start()
    part = nz // CHUNKS
    copies = []
    for k in range(CHUNKS):
        at = pl.ds(k * part, part)
        copies.append(pltpu.make_async_copy(q_ref.at[:, at], q_here.at[:, at], sems.at[k]))
        copies[k].start()
    lab_copy = pltpu.make_async_copy(lab_ref, lab_here, sems.at[CHUNKS + 1])
    lab_copy.start()
    lane = lax.broadcasted_iota(jnp.int32, (BLOCK, lanes), 1)
    zeros = jnp.zeros((PAD, lanes), jnp.float32)
    for z in range(nz):
        s_ref[z, 0:PAD, :] = zeros
        s_ref[z, PAD + rows:, :] = zeros

    src = lax.broadcasted_iota(jnp.int32, (lanes, 2 * lanes), 0)
    dst = lax.broadcasted_iota(jnp.int32, (lanes, 2 * lanes), 1)
    inside = (dst > 0) & (dst < lanes - 1)
    near = jnp.where(inside & (src == dst + 1), 1.0, 0.0) - jnp.where(inside & (src == dst - 1), 1.0, 0.0)
    odd = (dst & 1) == 1
    ends = jnp.where(odd & (src == 1), 1.0, 0.0) - jnp.where(odd, 0.0, jnp.where(src == lanes - 2, 1.0, 0.0))
    pick = jnp.where(dst < lanes, near, ends).astype(jnp.bfloat16)
    pick_ref[0:lanes, :] = pick
    pick_ref[lanes:, :] = pick

    nlab, nchan, nbins = tab_here.shape
    rows_tab[...] = jnp.zeros_like(rows_tab)
    tab_copy.wait()
    for lab in range(nlab):
        rows_tab[lab, 0:nchan, 0:nbins] = tab_here[lab]
    knots = rows_tab[0]
    for lab in range(1, nlab):
        knots = knots + pltpu.roll(rows_tab[lab], lab * nbins, 1)
    knots_ref[0] = knots
    knots_ref[1] = pltpu.roll(knots, lanes - 1, 1) - knots
    top = jnp.broadcast_to(jnp.max(knots, axis=1, keepdims=True), (SUB, lanes))
    cover = 1.0 - jnp.exp(-1.25 * step * nz * top[nchan - 1:nchan, :])
    row = lax.broadcasted_iota(jnp.int32, (SUB, lanes), 0)
    scale_ref[...] = jnp.where(row < nchan - 1, top, 1.0) * cover * MARGIN

    for k in range(CHUNKS):
        copies[k].wait()

        def block(i, carry, k=k):
            r0 = pl.multiple_of(i * BLOCK, BLOCK)
            packed = edge[pl.ds(r0, BLOCK), :]
            for z in range(k * part, (k + 1) * part):
                q = [q_here[c, z, pl.ds(r0, BLOCK), :].astype(jnp.float32) for c in range(5)]
                s = 3.0 * (q[0] * q[0] + q[3] * q[3] + q[0] * q[3] + q[1] * q[1] + q[2] * q[2] + q[4] * q[4])
                s_ref[z, pl.ds(r0 + PAD, BLOCK), :] = s
                if z == 0:
                    first_ref[pl.ds(r0, BLOCK), :] = encode(s, STRENGTH_MAX).astype(jnp.int16)
                if z == nz - 1:
                    last_ref[pl.ds(r0, BLOCK), :] = encode(s, STRENGTH_MAX).astype(jnp.int16)
                turned = pltpu.roll(s, 2 * z + 1, 1)
                packed = jnp.where(lane >> 1 == z, turned, packed)
            edge[pl.ds(r0, BLOCK), :] = packed
            return carry

        lax.fori_loop(0, rows // BLOCK, block, 0)
    edge_t[...] = edge[...].T
    odd = lax.axis_index("cols") % 2
    inner_ref[...] = edge_t[pl.ds(odd, nz, stride=2), :]
    outer_ref[...] = edge_t[pl.ds(1 - odd, nz, stride=2), :]
    lab_copy.wait()


def lookup_kernel(nbins, knots_ref, pick_ref, s_ref, lab_ref, value_ref, part_ref, edge_ref, dx_here):
    nz, rows, lanes = lab_ref.shape
    nchan = value_ref.shape[0]
    lane = lax.broadcasted_iota(jnp.int32, (rows, lanes), 1)
    base = [jnp.broadcast_to(knots_ref[0, k:k + 1, :], (SUB, lanes)) for k in range(nchan)]
    diff = [jnp.broadcast_to(knots_ref[1, k:k + 1, :], (SUB, lanes)) for k in range(nchan)]

    packed = jnp.zeros((rows, lanes), jnp.float32)
    for z in range(nz):
        layer = s_ref[z, PAD:PAD + rows, :]
        high = layer.astype(jnp.bfloat16)
        low = (layer - high.astype(jnp.float32)).astype(jnp.bfloat16)
        both = jnp.dot(jnp.concatenate([high, low], axis=1), pick_ref[...], preferred_element_type=jnp.float32)
        dx_here[z] = both[:, :lanes]
        packed = jnp.where(lane >> 1 == z, both[:, lanes:], packed)
    edge_ref[...] = packed

    def block(i, carry):
        r0 = pl.multiple_of(i * SUB, SUB)
        at = pl.ds(r0, SUB)
        below = None
        here = s_ref[0, pl.ds(r0 + PAD, SUB), :]
        for z in range(nz):
            above = s_ref[z + 1, pl.ds(r0 + PAD, SUB), :] if z < nz - 1 else None
            dx = dx_here[z, at, :]
            dy = s_ref[z, pl.ds(r0 + PAD + 1, SUB), :] - s_ref[z, pl.ds(r0 + PAD - 1, SUB), :]
            part = dy * dy + dx * dx
            if 0 < z < nz - 1:
                dz = above - below
                part = part + dz * dz
            part_ref[z, at, :] = part
            coord = jnp.clip(2.0 * here, 0.0, nbins - 1.0)
            knot = coord.astype(jnp.int32)
            frac = coord - knot.astype(jnp.float32)
            index = lab_ref[z, at, :] * nbins + knot
            for chan in range(nchan):
                low = jnp.take_along_axis(base[chan], index, axis=1, mode="promise_in_bounds")
                rise = jnp.take_along_axis(diff[chan], index, axis=1, mode="promise_in_bounds")
                value_ref[chan, z, at, :] = low + frac * rise
            below, here = here, above
        return carry

    lax.fori_loop(0, rows // SUB, block, 0, unroll=16)


def most_kernel(step, value_ref, part_ref, edge_ref, s_ref, before_ref, swap1_ref, swap0_ref,
                state_ref, slope_ref, halo, halo_t, below_here):
    _, nz, rows, lanes = value_ref.shape
    d = lax.axis_index("depth")
    c = lax.axis_index("cols")
    has_before = (d > 0).astype(jnp.float32)
    has_left = (c > 0).astype(jnp.float32)
    has_right = (c < lax.axis_size("cols") - 1).astype(jnp.float32)
    lane = lax.broadcasted_iota(jnp.int32, (SUB, lanes), 1)
    outer = (lane == 0) | (lane == lanes - 1)

    odd = c % 2 == 1
    left = jnp.where(odd, swap0_ref[...], swap1_ref[...])
    right = jnp.where(odd, swap1_ref[...], swap0_ref[...])
    halo[pl.ds(0, nz, stride=2), :] = right * has_right
    halo[pl.ds(1, nz, stride=2), :] = -left * has_left
    halo_t[...] = halo[...].T
    below_here[...] = decode(before_ref[...].astype(jnp.int32), STRENGTH_MAX) * has_before


    def block(i, carry):
        r0 = pl.multiple_of(i * SUB, SUB)
        at = pl.ds(r0, SUB)
        inside = pl.ds(r0 + PAD, SUB)
        sides = halo_t[at, :] + edge_ref[at, :]
        sides = sides * sides
        transmit = jnp.ones((SUB, lanes), jnp.float32)
        colors = [jnp.zeros((SUB, lanes), jnp.float32) for _ in range(3)]
        for z in range(nz):
            slope4 = part_ref[z, at, :] + jnp.where(outer, pltpu.roll(sides, lanes - 1 - 2 * z, 1), 0.0)
            if z == 0:
                dz = s_ref[1, inside, :] - below_here[at, :]
                slope4 = slope4 + dz * dz
            if z == nz - 1:
                slope_ref[at, :] = slope4
                break
            extinction = value_ref[3, z, at, :] * (1.25 - 4.0 / (4.0 + slope4))
            passed = transmit * jnp.exp(-step * extinction)
            weight = transmit - passed
            for chan in range(3):
                colors[chan] = colors[chan] + weight * value_ref[chan, z, at, :]
            transmit = passed
        for k, v in enumerate(colors + [transmit]):
            state_ref[i, k] = v
        return carry

    lax.fori_loop(0, rows // SUB, block, 0, unroll=16)


def last_kernel(step, scale_ref, state_ref, slope_ref, value_ref, s_ref, after_ref, out_ref, above_here):
    _, nz, rows, lanes = value_ref.shape
    has_after = (lax.axis_index("depth") < lax.axis_size("depth") - 1).astype(jnp.float32)
    above_here[...] = decode(after_ref[...].astype(jnp.int32), STRENGTH_MAX) * has_after
    scale = [jnp.broadcast_to(scale_ref[k:k + 1, :], (SUB, lanes)) for k in range(4)]

    def block(i, carry):
        r0 = pl.multiple_of(i * SUB, SUB)
        at = pl.ds(r0, SUB)
        dz = above_here[at, :] - s_ref[nz - 2, pl.ds(r0 + PAD, SUB), :]
        slope4 = slope_ref[at, :] + dz * dz
        extinction = value_ref[3, nz - 1, at, :] * (1.25 - 4.0 / (4.0 + slope4))
        transmit = state_ref[i, 3]
        passed = transmit * jnp.exp(-step * extinction)
        weight = transmit - passed
        colors = [state_ref[i, chan] + weight * value_ref[chan, nz - 1, at, :] for chan in range(3)]
        sent = [encode(v, scale[k]) for k, v in enumerate(colors + [1.0 - passed])]
        out_ref[i, 0] = jnp.concatenate(sent[:2], axis=0).astype(jnp.int16)
        out_ref[i, 1] = jnp.concatenate(sent[2:], axis=0).astype(jnp.int16)
        return carry

    lax.fori_loop(0, rows // SUB, block, 0, unroll=16)


def combine_kernel(scale_ref, slab_ref, out_ref):
    count, _, _, lanes = slab_ref.shape
    scale = [jnp.broadcast_to(scale_ref[k:k + 1, :], (SUB, lanes)) for k in range(4)]
    transmit = jnp.ones((SUB, lanes), jnp.float32)
    colors = [jnp.zeros((SUB, lanes), jnp.float32)] * 3
    for k in range(count):
        pairs = [slab_ref[k, j].astype(jnp.int32) for j in range(2)]
        came = [decode(pairs[c // 2][c % 2 * SUB:(c % 2 + 1) * SUB], scale[c]) for c in range(4)]
        for chan in range(3):
            colors[chan] = colors[chan] + transmit * came[chan]
        transmit = transmit * (1.0 - came[3])
    for chan in range(3):
        out_ref[chan] = colors[chan]
    out_ref[3] = 1.0 - transmit


def on_device(qtensor, labels, tables):
    _, nz, rows, lanes = qtensor.shape
    groups = lax.axis_size("depth")
    across = lax.axis_size("cols")
    step = 2.0 / (nz * groups)
    params = pltpu.CompilerParams(vmem_limit_bytes=32 * 1024 * 1024)
    f32 = lambda *shape: jax.ShapeDtypeStruct(shape, jnp.float32)
    layer = f32(rows, lanes)
    coded = jax.ShapeDtypeStruct((rows, lanes), jnp.int16)
    column = f32(nz, rows)
    plane = pltpu.VMEM((rows, lanes), jnp.float32)
    nlab, nchan, nbins = tables.shape
    far = lambda array: pltpu.with_memory_space_constraint(array, pltpu.HBM)
    s, first, last, to_inner, to_outer, labels, knots, scale, pick = pl.pallas_call(
        functools.partial(strength_kernel, step),
        in_specs=[pl.BlockSpec(memory_space=pltpu.HBM)] * 3,
        out_shape=[
            f32(nz, rows + 2 * PAD, lanes), coded, coded, column, column,
            jax.ShapeDtypeStruct(labels.shape, labels.dtype), f32(2, SUB, lanes), f32(SUB, lanes),
            jax.ShapeDtypeStruct((2 * lanes, 2 * lanes), jnp.bfloat16),
        ],
        scratch_shapes=[
            pltpu.VMEM(qtensor.shape, qtensor.dtype),
            pltpu.SemaphoreType.DMA((CHUNKS + 2,)),
            pltpu.VMEM(tables.shape, jnp.float32),
            pltpu.VMEM((nlab, SUB, lanes), jnp.float32),
            plane,
            pltpu.VMEM((lanes, rows), jnp.float32),
        ],
        compiler_params=params,
        name="strength",
    )(far(qtensor), far(labels), far(tables))

    up = lambda n: [(i, (i + 1) % n) for i in range(n)]
    down = lambda n: [(i, (i - 1) % n) for i in range(n)]
    after = lax.ppermute(first, "depth", down(groups))
    before = lax.ppermute(last, "depth", up(groups))
    inner = [(i, i ^ 1) for i in range(across)]
    outer = []
    for i in range(across):
        j = ((i + 1) ^ 1) - 1
        for g in range(groups):
            outer.append((i * groups + g, j * groups + g if 0 <= j < across else i * groups + (g ^ groups // 4)))
    swap0 = lax.ppermute(to_inner, "cols", inner)
    swap1 = lax.ppermute(to_outer, ("cols", "depth"), outer)

    value, part, edge = pl.pallas_call(
        functools.partial(lookup_kernel, nbins),
        out_shape=[f32(nchan, nz, rows, lanes), f32(nz, rows, lanes), layer],
        scratch_shapes=[pltpu.VMEM((nz, rows, lanes), jnp.float32)],
        compiler_params=params,
        cost_estimate=pl.CostEstimate(flops=60 * nz * rows * lanes, bytes_accessed=28 * nz * rows * lanes, transcendentals=0),
        name="lookup",
    )(knots, pick, s, labels)

    state, slope = pl.pallas_call(
        functools.partial(most_kernel, step),
        out_shape=[f32(rows // SUB, 4, SUB, lanes), layer],
        scratch_shapes=[pltpu.VMEM((lanes, rows), jnp.float32), plane, plane],
        compiler_params=params,
        name="most",
    )(value, part, edge, s, before, swap1, swap0)
    slabs = pl.pallas_call(
        functools.partial(last_kernel, step),
        out_shape=jax.ShapeDtypeStruct((rows // SUB, 2, 2 * SUB, lanes), jnp.int16),
        scratch_shapes=[plane],
        compiler_params=params,
        name="last",
    )(scale, state, slope, value, s, after)

    mine = lax.all_to_all(slabs, "depth", 0, 0)
    return pl.pallas_call(
        combine_kernel, out_shape=f32(4, SUB, lanes), compiler_params=params, name="combine"
    )(scale, mine)


def solution(mesh):
    placed = (P(None, "depth", None, "cols"), P("depth", None, "cols"), P())
    return jax.shard_map(
        on_device, mesh=mesh, in_specs=placed, out_specs=P(None, "depth", "cols"), check_vma=False
    )
```

```python
import functools
import jax
import jax.numpy as jnp
from jax import lax
from jax.experimental import pallas as pl
from jax.experimental.pallas import tpu as pltpu
from jax.sharding import PartitionSpec as P

SUB = 8
PAD = 8
CHUNKS = 2
BLOCK = 128
LEVELS = 65535.0
MIDDLE = 32768
MARGIN = 1.0001
STRENGTH_MAX = 3.0 * 6.0 * 2.5 * 2.5 * MARGIN


def encode(value, inverse):
    level = jnp.sqrt(jnp.clip(value * inverse, 0.0, 1.0)) * LEVELS + 0.5
    return level.astype(jnp.int32) - MIDDLE


def decode(level, scale):
    root = (level + MIDDLE).astype(jnp.float32) * (1.0 / LEVELS)
    return root * root * scale


def strength_kernel(step, q_ref, lab_ref, tab_ref, s_ref, first_ref, last_ref, inner_ref, outer_ref, lab_here, knots_ref, scale_ref, pick_ref, q_here, sems, tab_here, rows_tab, edge, edge_t):
    _, nz, rows, lanes = q_here.shape
    tab_copy = pltpu.make_async_copy(tab_ref, tab_here, sems.at[CHUNKS])
    tab_copy.start()
    part = nz // CHUNKS
    copies = []
    for k in range(CHUNKS):
        at = pl.ds(k * part, part)
        copies.append(pltpu.make_async_copy(q_ref.at[:, at], q_here.at[:, at], sems.at[k]))
        copies[k].start()
    lab_copy = pltpu.make_async_copy(lab_ref, lab_here, sems.at[CHUNKS + 1])
    lab_copy.start()
    lane = lax.broadcasted_iota(jnp.int32, (BLOCK, lanes), 1)
    zeros = jnp.zeros((PAD, lanes), jnp.float32)
    for z in range(nz):
        s_ref[z, 0:PAD, :] = zeros
        s_ref[z, PAD + rows:, :] = zeros

    src = lax.broadcasted_iota(jnp.int32, (lanes, 2 * lanes), 0)
    dst = lax.broadcasted_iota(jnp.int32, (lanes, 2 * lanes), 1)
    inside = (dst > 0) & (dst < lanes - 1)
    near = jnp.where(inside & (src == dst + 1), 1.0, 0.0) - jnp.where(inside & (src == dst - 1), 1.0, 0.0)
    odd = (dst & 1) == 1
    ends = jnp.where(odd & (src == 1), 1.0, 0.0) - jnp.where(odd, 0.0, jnp.where(src == lanes - 2, 1.0, 0.0))
    pick = jnp.where(dst < lanes, near, ends).astype(jnp.bfloat16)
    pick_ref[0:lanes, :] = pick
    pick_ref[lanes:, :] = pick

    nlab, nchan, nbins = tab_here.shape
    rows_tab[...] = jnp.zeros_like(rows_tab)
    tab_copy.wait()
    for lab in range(nlab):
        rows_tab[lab, 0:nchan, 0:nbins] = tab_here[lab]
    knots = rows_tab[0]
    for lab in range(1, nlab):
        knots = knots + pltpu.roll(rows_tab[lab], lab * nbins, 1)
    knots_ref[0] = knots
    knots_ref[1] = pltpu.roll(knots, lanes - 1, 1) - knots
    top = jnp.broadcast_to(jnp.max(knots, axis=1, keepdims=True), (SUB, lanes))
    cover = 1.0 - jnp.exp(-1.25 * step * nz * top[nchan - 1:nchan, :])
    row = lax.broadcasted_iota(jnp.int32, (SUB, lanes), 0)
    scale_ref[...] = jnp.where(row < nchan - 1, top, 1.0) * cover * MARGIN

    for k in range(CHUNKS):
        copies[k].wait()

        def block(i, carry, k=k):
            r0 = pl.multiple_of(i * BLOCK, BLOCK)
            packed = edge[pl.ds(r0, BLOCK), :]
            for z in range(k * part, (k + 1) * part):
                q = [q_here[c, z, pl.ds(r0, BLOCK), :].astype(jnp.float32) for c in range(5)]
                s = 3.0 * (q[0] * q[0] + q[3] * q[3] + q[0] * q[3] + q[1] * q[1] + q[2] * q[2] + q[4] * q[4])
                s_ref[z, pl.ds(r0 + PAD, BLOCK), :] = s
                if z == 0:
                    first_ref[pl.ds(r0, BLOCK), :] = encode(s, 1.0 / STRENGTH_MAX).astype(jnp.int16)
                if z == nz - 1:
                    last_ref[pl.ds(r0, BLOCK), :] = encode(s, 1.0 / STRENGTH_MAX).astype(jnp.int16)
                turned = pltpu.roll(s, 2 * z + 1, 1)
                packed = jnp.where(lane >> 1 == z, turned, packed)
            edge[pl.ds(r0, BLOCK), :] = packed
            return carry

        lax.fori_loop(0, rows // BLOCK, block, 0)
    edge_t[...] = edge[...].T
    odd = lax.axis_index("cols") % 2
    inner_ref[...] = edge_t[pl.ds(odd, nz, stride=2), :]
    outer_ref[...] = edge_t[pl.ds(1 - odd, nz, stride=2), :]
    lab_copy.wait()


def lookup_kernel(nbins, knots_ref, pick_ref, s_ref, lab_ref, value_ref, part_ref, edge_ref, dx_here):
    nz, rows, lanes = lab_ref.shape
    nchan = value_ref.shape[0]
    lane = lax.broadcasted_iota(jnp.int32, (rows, lanes), 1)
    base = [jnp.broadcast_to(knots_ref[0, k:k + 1, :], (SUB, lanes)) for k in range(nchan)]
    diff = [jnp.broadcast_to(knots_ref[1, k:k + 1, :], (SUB, lanes)) for k in range(nchan)]

    packed = jnp.zeros((rows, lanes), jnp.float32)
    for z in range(nz):
        layer = s_ref[z, PAD:PAD + rows, :]
        high = layer.astype(jnp.bfloat16)
        low = (layer - high.astype(jnp.float32)).astype(jnp.bfloat16)
        both = jnp.dot(jnp.concatenate([high, low], axis=1), pick_ref[...], preferred_element_type=jnp.float32)
        dx_here[z] = both[:, :lanes]
        packed = jnp.where(lane >> 1 == z, both[:, lanes:], packed)
    edge_ref[...] = packed

    def block(i, carry):
        r0 = pl.multiple_of(i * SUB, SUB)
        at = pl.ds(r0, SUB)
        below = None
        here = s_ref[0, pl.ds(r0 + PAD, SUB), :]
        for z in range(nz):
            above = s_ref[z + 1, pl.ds(r0 + PAD, SUB), :] if z < nz - 1 else None
            dx = dx_here[z, at, :]
            dy = s_ref[z, pl.ds(r0 + PAD + 1, SUB), :] - s_ref[z, pl.ds(r0 + PAD - 1, SUB), :]
            part = dy * dy + dx * dx
            if 0 < z < nz - 1:
                dz = above - below
                part = part + dz * dz
            part_ref[z, at, :] = part
            coord = jnp.clip(2.0 * here, 0.0, nbins - 1.0)
            knot = coord.astype(jnp.int32)
            frac = coord - knot.astype(jnp.float32)
            index = lab_ref[z, at, :] * nbins + knot
            for chan in range(nchan):
                low = jnp.take_along_axis(base[chan], index, axis=1, mode="promise_in_bounds")
                rise = jnp.take_along_axis(diff[chan], index, axis=1, mode="promise_in_bounds")
                value_ref[chan, z, at, :] = low + frac * rise
            below, here = here, above
        return carry

    lax.fori_loop(0, rows // SUB, block, 0, unroll=16)


def most_kernel(step, value_ref, part_ref, edge_ref, s_ref, before_ref, swap1_ref, swap0_ref,
                state_ref, slope_ref, halo, halo_t, below_here):
    _, nz, rows, lanes = value_ref.shape
    d = lax.axis_index("depth")
    c = lax.axis_index("cols")
    has_before = (d > 0).astype(jnp.float32)
    has_left = (c > 0).astype(jnp.float32)
    has_right = (c < lax.axis_size("cols") - 1).astype(jnp.float32)
    lane = lax.broadcasted_iota(jnp.int32, (SUB, lanes), 1)
    outer = (lane == 0) | (lane == lanes - 1)

    odd = c % 2 == 1
    left = jnp.where(odd, swap0_ref[...], swap1_ref[...])
    right = jnp.where(odd, swap1_ref[...], swap0_ref[...])
    halo[pl.ds(0, nz, stride=2), :] = right * has_right
    halo[pl.ds(1, nz, stride=2), :] = -left * has_left
    halo_t[...] = halo[...].T
    below_here[...] = decode(before_ref[...].astype(jnp.int32), STRENGTH_MAX) * has_before


    def block(i, carry):
        r0 = pl.multiple_of(i * SUB, SUB)
        at = pl.ds(r0, SUB)
        inside = pl.ds(r0 + PAD, SUB)
        sides = halo_t[at, :] + edge_ref[at, :]
        sides = sides * sides
        transmit = jnp.ones((SUB, lanes), jnp.float32)
        colors = [jnp.zeros((SUB, lanes), jnp.float32) for _ in range(3)]
        for z in range(nz):
            slope4 = part_ref[z, at, :] + jnp.where(outer, pltpu.roll(sides, lanes - 1 - 2 * z, 1), 0.0)
            if z == 0:
                dz = s_ref[1, inside, :] - below_here[at, :]
                slope4 = slope4 + dz * dz
            if z == nz - 1:
                slope_ref[at, :] = slope4
                break
            extinction = value_ref[3, z, at, :] * (1.25 - 4.0 / (4.0 + slope4))
            passed = transmit * jnp.exp(-step * extinction)
            weight = transmit - passed
            for chan in range(3):
                colors[chan] = colors[chan] + weight * value_ref[chan, z, at, :]
            transmit = passed
        for k, v in enumerate(colors + [transmit]):
            state_ref[i, k] = v
        return carry

    lax.fori_loop(0, rows // SUB, block, 0, unroll=16)


def last_kernel(step, scale_ref, state_ref, slope_ref, value_ref, s_ref, after_ref, out_ref, above_here):
    _, nz, rows, lanes = value_ref.shape
    has_after = (lax.axis_index("depth") < lax.axis_size("depth") - 1).astype(jnp.float32)
    above_here[...] = decode(after_ref[...].astype(jnp.int32), STRENGTH_MAX) * has_after
    bound = 1.0 / scale_ref[...]
    inverse = [jnp.broadcast_to(bound[k:k + 1, :], (SUB, lanes)) for k in range(4)]

    def block(i, carry):
        r0 = pl.multiple_of(i * SUB, SUB)
        at = pl.ds(r0, SUB)
        dz = above_here[at, :] - s_ref[nz - 2, pl.ds(r0 + PAD, SUB), :]
        slope4 = slope_ref[at, :] + dz * dz
        extinction = value_ref[3, nz - 1, at, :] * (1.25 - 4.0 / (4.0 + slope4))
        transmit = state_ref[i, 3]
        passed = transmit * jnp.exp(-step * extinction)
        weight = transmit - passed
        colors = [state_ref[i, chan] + weight * value_ref[chan, nz - 1, at, :] for chan in range(3)]
        sent = [encode(v, inverse[k]) for k, v in enumerate(colors + [1.0 - passed])]
        out_ref[i, 0] = jnp.concatenate(sent[:2], axis=0).astype(jnp.int16)
        out_ref[i, 1] = jnp.concatenate(sent[2:], axis=0).astype(jnp.int16)
        return carry

    lax.fori_loop(0, rows // SUB, block, 0, unroll=16)


def combine_kernel(scale_ref, slab_ref, out_ref):
    count, _, _, lanes = slab_ref.shape
    scale = [jnp.broadcast_to(scale_ref[k:k + 1, :], (SUB, lanes)) for k in range(4)]
    transmit = jnp.ones((SUB, lanes), jnp.float32)
    colors = [jnp.zeros((SUB, lanes), jnp.float32)] * 3
    for k in range(count):
        pairs = [slab_ref[k, j].astype(jnp.int32) for j in range(2)]
        came = [decode(pairs[c // 2][c % 2 * SUB:(c % 2 + 1) * SUB], scale[c]) for c in range(4)]
        for chan in range(3):
            colors[chan] = colors[chan] + transmit * came[chan]
        transmit = transmit * (1.0 - came[3])
    for chan in range(3):
        out_ref[chan] = colors[chan]
    out_ref[3] = 1.0 - transmit


def on_device(qtensor, labels, tables):
    _, nz, rows, lanes = qtensor.shape
    groups = lax.axis_size("depth")
    across = lax.axis_size("cols")
    step = 2.0 / (nz * groups)
    params = pltpu.CompilerParams(vmem_limit_bytes=32 * 1024 * 1024)
    f32 = lambda *shape: jax.ShapeDtypeStruct(shape, jnp.float32)
    layer = f32(rows, lanes)
    coded = jax.ShapeDtypeStruct((rows, lanes), jnp.int16)
    column = f32(nz, rows)
    plane = pltpu.VMEM((rows, lanes), jnp.float32)
    nlab, nchan, nbins = tables.shape
    far = lambda array: pltpu.with_memory_space_constraint(array, pltpu.HBM)
    s, first, last, to_inner, to_outer, labels, knots, scale, pick = pl.pallas_call(
        functools.partial(strength_kernel, step),
        in_specs=[pl.BlockSpec(memory_space=pltpu.HBM)] * 3,
        out_shape=[
            f32(nz, rows + 2 * PAD, lanes), coded, coded, column, column,
            jax.ShapeDtypeStruct(labels.shape, labels.dtype), f32(2, SUB, lanes), f32(SUB, lanes),
            jax.ShapeDtypeStruct((2 * lanes, 2 * lanes), jnp.bfloat16),
        ],
        scratch_shapes=[
            pltpu.VMEM(qtensor.shape, qtensor.dtype),
            pltpu.SemaphoreType.DMA((CHUNKS + 2,)),
            pltpu.VMEM(tables.shape, jnp.float32),
            pltpu.VMEM((nlab, SUB, lanes), jnp.float32),
            plane,
            pltpu.VMEM((lanes, rows), jnp.float32),
        ],
        compiler_params=params,
        name="strength",
    )(far(qtensor), far(labels), far(tables))

    up = lambda n: [(i, (i + 1) % n) for i in range(n)]
    down = lambda n: [(i, (i - 1) % n) for i in range(n)]
    after = lax.ppermute(first, "depth", down(groups))
    before = lax.ppermute(last, "depth", up(groups))
    inner = [(i, i ^ 1) for i in range(across)]
    outer = []
    for i in range(across):
        j = ((i + 1) ^ 1) - 1
        for g in range(groups):
            outer.append((i * groups + g, j * groups + g if 0 <= j < across else i * groups + (g ^ groups // 4)))
    swap0 = lax.ppermute(to_inner, "cols", inner)
    swap1 = lax.ppermute(to_outer, ("cols", "depth"), outer)

    value, part, edge = pl.pallas_call(
        functools.partial(lookup_kernel, nbins),
        out_shape=[f32(nchan, nz, rows, lanes), f32(nz, rows, lanes), layer],
        scratch_shapes=[pltpu.VMEM((nz, rows, lanes), jnp.float32)],
        compiler_params=params,
        cost_estimate=pl.CostEstimate(flops=60 * nz * rows * lanes, bytes_accessed=28 * nz * rows * lanes, transcendentals=0),
        name="lookup",
    )(knots, pick, s, labels)

    state, slope = pl.pallas_call(
        functools.partial(most_kernel, step),
        out_shape=[f32(rows // SUB, 4, SUB, lanes), layer],
        scratch_shapes=[pltpu.VMEM((lanes, rows), jnp.float32), plane, plane],
        compiler_params=params,
        name="most",
    )(value, part, edge, s, before, swap1, swap0)
    slabs = pl.pallas_call(
        functools.partial(last_kernel, step),
        out_shape=jax.ShapeDtypeStruct((rows // SUB, 2, 2 * SUB, lanes), jnp.int16),
        scratch_shapes=[plane],
        compiler_params=params,
        name="last",
    )(scale, state, slope, value, s, after)

    mine = lax.all_to_all(slabs, "depth", 0, 0)
    return pl.pallas_call(
        combine_kernel, out_shape=f32(4, SUB, lanes), compiler_params=params, name="combine"
    )(scale, mine)


def solution(mesh):
    placed = (P(None, "depth", None, "cols"), P("depth", None, "cols"), P())
    return jax.shard_map(
        on_device, mesh=mesh, in_specs=placed, out_specs=P(None, "depth", "cols"), check_vma=False
    )
```
